512 devices in a mesh: segment: 2 (over y_hi), dp: 64 (over z, x, core), rows: 4 (over y_lo).
Axes of the slice: x: 4, y: 8 (y_hi: 2, y_lo: 4; y = y_hi * 4 + y_lo), z: 8, core: 2. Of those that a mesh axis runs over, the one named last changes fastest.
Arguments:
- section_input: bfloat16 [2, 2, 64, 20, 16, 1536], P('segment', None, 'dp', 'rows'), may hold values from -16 to 16
- adjoint_in: bfloat16 [2, 64, 20, 16, 1536], P(None, 'dp', 'rows'), may hold values from -6 to 6
- kernel: bfloat16 [2, 1, 49, 1536], P('segment', None, None, 'dp'), may hold values from -0.875 to 0.875
- conv_bias: bfloat16 [2, 1, 1536], P('segment', None, 'dp'), may hold values from -4 to 4
- ln_gain: bfloat16 [2, 1, 1536], P('segment', None, 'dp'), may hold values from 0.099609375 to 1.8984375
- ln_shift: bfloat16 [2, 1, 1536], P('segment', None, 'dp'), may hold values from -3 to 3
- layer_scale: bfloat16 [2, 1, 1536], P('segment', None, 'dp'), may hold values from 0.29882812 to 1.5
Outputs:
- section_adjoint: bfloat16 [2, 2, 64, 20, 16, 1536], P('segment', None, 'dp', 'rows')
- kernel_grad: float32 [2, 1, 49, 1536], P('segment', None, None, 'dp')
- bias_grad: float32 [2, 1, 1536], P('segment', None, 'dp')
- gain_grad: float32 [2, 1, 1536], P('segment', None, 'dp')
- shift_grad: float32 [2, 1, 1536], P('segment', None, 'dp')
- scale_grad: float32 [2, 1, 1536], P('segment', None, 'dp')
The draws below stay inside these ranges and needn't reach their ends.
All inputs are finite; a program needn't handle non-finite values.
Results may differ from the reference program's by a relative error of at most 0.005.
Values may be sent and summed in bfloat16 or wider, within the bound.
A program may use at most 64 MiB of HBM per device.

```python
import math
import jax
import jax.numpy as jnp
from jax import lax

C = 1536
IMAGE_ROWS = 20
COLS = 16
MICRO = 2
LAYERS = 1
BATCH = 64
SEGMENTS = 2


def with_spikes(result, stream_key, source, target, shards_of, factor):
    owner, partner = [(jnp.arange(result.shape[axis_at]) // (result.shape[axis_at] // shards_of)).reshape([-1 if axis == axis_at else 1 for axis in range(result.ndim)]) for axis_at in (source, target)]
    chosen = jax.random.permutation(stream_key, shards_of)[partner]
    strong = (owner == chosen) | (owner == (partner + shards_of // 2) % shards_of)
    return jnp.where(strong, factor * result, result)


def levels(key, extent, pieces, low, top_value):
    loudness, own = 1.0, jax.random.fold_in(key, 6)
    for dim, shards_of in pieces:
        draws = jnp.exp(jax.random.uniform(jax.random.fold_in(own, dim), (shards_of,), jnp.float32, low / len(pieces), top_value / len(pieces)))
        loudness = loudness * jnp.repeat(draws, extent[dim] // shards_of).reshape([-1 if axis == dim else 1 for axis in range(len(extent))])
    return loudness


def noise(key, extent, scale, most, cuts=(), kind=jnp.bfloat16):
    gain = levels(key, extent, cuts, -0.22, 0.18) if cuts else 1.0
    array = jax.random.normal(key, extent, jnp.float32) * scale * gain
    return jnp.minimum(jnp.maximum(array, -most), most).astype(kind)


def bell_draw_with(own_key, shape, scale, reach, shards, heavy, held_as=jnp.bfloat16):
    values = scale * jax.random.normal(own_key, shape, jnp.float32)
    if shards:
        values = values * levels(own_key, shape, shards, -0.22, 0.18)
    return jnp.clip(with_spikes(values, jax.random.fold_in(own_key, 3), *heavy), -reach, reach).astype(held_as)


def setup_inputs(seed: int = 0) -> dict:
    seeds = jax.random.split(jax.random.key(seed), 8)
    return {
        "section_input": bell_draw_with(seeds[0], (SEGMENTS, MICRO, BATCH, IMAGE_ROWS, COLS, C), 1.0, 16.0, ((0, 2), (2, 64), (3, 4)), (2, 5, 64, 4.0)),
        "adjoint_in": noise(seeds[1], (MICRO, BATCH, IMAGE_ROWS, COLS, C), 1.0, 6.0, ((1, 64), (2, 4))),
        "kernel": noise(seeds[2], (SEGMENTS, LAYERS, 49, C), 49 ** -0.5, 0.875, ((0, 2), (3, 64))),
        "conv_bias": noise(seeds[3], (SEGMENTS, LAYERS, C), 1.0, 4.0, ((0, 2), (2, 64))),
        "ln_gain": jnp.clip(1.0 + 0.18 * jax.random.normal(seeds[4], (SEGMENTS, LAYERS, C), jnp.float32), 0.099609375, 1.8984375).astype(jnp.bfloat16),
        "ln_shift": noise(seeds[5], (SEGMENTS, LAYERS, C), 0.5, 3.0, ((0, 2), (2, 64))),
        "layer_scale": jnp.clip(jnp.exp(math.log(1.5) - 1.6133518 * jax.random.uniform(seeds[6], (SEGMENTS, LAYERS, C), jnp.float32) ** levels(seeds[6], (SEGMENTS, LAYERS, C), ((0, 2), (2, 64)), -0.2, 0.2)), 0.29882812, 1.5).astype(jnp.bfloat16),
    }


EPSILON = 1e-06

def conv_sum(padded, kernel, height, width):
    total = jnp.zeros((padded.shape[0], height, width, padded.shape[3]), jnp.float32)
    for row_off in range(7):
        for col_off in range(7):
            total = total + padded[:, row_off:row_off + height, col_off:col_off + width, :] * kernel[row_off * 7 + col_off]
    return total

def conv_adjoint(grad_pad, kernel, height, width):
    total = jnp.zeros((grad_pad.shape[0], height, width, grad_pad.shape[3]), jnp.float32)
    for row_off in range(7):
        for col_off in range(7):
            total = total + grad_pad[:, 6 - row_off:6 - row_off + height, 6 - col_off:6 - col_off + width, :] * kernel[row_off * 7 + col_off]
    return total

def kernel_terms(padded, grad_float, height, width):
    return jnp.stack([lax.optimization_barrier(jnp.sum(padded[:, row_off:row_off + height, col_off:col_off + width, :] * grad_float, axis=(0, 1, 2))) for row_off in range(7) for col_off in range(7)])

def statistics(padded, kernel, conv_bias, ln_gain, ln_shift, height, width):
    mixed = conv_sum(padded, kernel.astype(jnp.float32), height, width) + conv_bias.astype(jnp.float32)
    average = lax.optimization_barrier(jnp.mean(mixed, axis=-1, keepdims=True))
    centred = mixed - average
    inverse = lax.rsqrt(lax.optimization_barrier(jnp.mean(centred * centred, axis=-1, keepdims=True)) + EPSILON)
    normed = centred * inverse
    shaped = normed * ln_gain.astype(jnp.float32) + ln_shift.astype(jnp.float32)
    return (normed, inverse, shaped)

def back_local(grad_out, normed, inverse, shaped, ln_gain, layer_scale):
    upstream = grad_out.astype(jnp.float32)
    grad_scale = lax.optimization_barrier(jnp.sum(shaped * upstream, axis=(0, 1, 2)))
    grad_shaped = layer_scale.astype(jnp.float32) * upstream
    grad_shift = lax.optimization_barrier(jnp.sum(grad_shaped, axis=(0, 1, 2)))
    grad_gain = lax.optimization_barrier(jnp.sum(grad_shaped * normed, axis=(0, 1, 2)))
    grad_normed = grad_shaped * ln_gain.astype(jnp.float32)
    grad_mix = inverse * (grad_normed - lax.optimization_barrier(jnp.mean(grad_normed, axis=-1, keepdims=True)) - normed * lax.optimization_barrier(jnp.mean(grad_normed * normed, axis=-1, keepdims=True)))
    grad_rounded = lax.optimization_barrier(grad_mix.astype(jnp.bfloat16))
    return (upstream, grad_rounded, grad_gain, grad_shift, grad_scale)

def pad_image(field):
    return jnp.pad(field.astype(jnp.float32), ((0, 0), (3, 3), (3, 3), (0, 0)))

def section_back(start, grad_out, kernel, conv_bias, ln_gain, ln_shift, layer_scale):
    height, width = (start.shape[1], start.shape[2])
    current = start
    saved = []
    for layer in range(LAYERS):
        padded = pad_image(current)
        normed, inverse, shaped = statistics(padded, kernel[layer], conv_bias[layer], ln_gain[layer], ln_shift[layer], height, width)
        saved.append((padded, normed, inverse, shaped))
        if layer + 1 < LAYERS:
            current = (current.astype(jnp.float32) + layer_scale[layer].astype(jnp.float32) * shaped).astype(jnp.bfloat16)
    found = [None] * LAYERS
    for layer in reversed(range(LAYERS)):
        padded, normed, inverse, shaped = saved[layer]
        upstream, grad_rounded, grad_gain, grad_shift, grad_scale = back_local(grad_out, normed, inverse, shaped, ln_gain[layer], layer_scale[layer])
        grad_float = grad_rounded.astype(jnp.float32)
        grad_bias = lax.optimization_barrier(jnp.sum(grad_float, axis=(0, 1, 2)))
        grad_kernel = kernel_terms(padded, grad_float, height, width)
        grad_pad = pad_image(grad_rounded)
        grad_out = (upstream + conv_adjoint(grad_pad, kernel[layer].astype(jnp.float32), height, width)).astype(jnp.bfloat16)
        found[layer] = (grad_kernel, grad_bias, grad_gain, grad_shift, grad_scale)
    stacked = tuple((jnp.stack([found[layer][which] for layer in range(LAYERS)]) for which in range(5)))
    return (grad_out, stacked)

def reference(section_input, adjoint_in, kernel, conv_bias, ln_gain, ln_shift, layer_scale):
    segments = section_input.shape[0]
    channels = kernel.shape[3]
    initial = (jnp.zeros((segments, LAYERS, 49, channels), jnp.float32),) + tuple((jnp.zeros((segments, LAYERS, channels), jnp.float32) for which in range(4)))

    def one_micro(carry, micro_idx):
        grad_out = lax.dynamic_index_in_dim(adjoint_in, micro_idx, 0, keepdims=False)
        results = [None] * segments
        segment_grads = [None] * segments
        for segment_idx in reversed(range(segments)):
            start = lax.dynamic_index_in_dim(section_input[segment_idx], micro_idx, 0, keepdims=False)
            grad_out, grads = section_back(start, grad_out, kernel[segment_idx], conv_bias[segment_idx], ln_gain[segment_idx], ln_shift[segment_idx], layer_scale[segment_idx])
            results[segment_idx] = grad_out
            segment_grads[segment_idx] = grads
        updated = tuple((carry[which] + jnp.stack([segment_grads[segment_idx][which] for segment_idx in range(segments)]) for which in range(5)))
        return (updated, jnp.stack(results))
    totals, adjoints = lax.scan(one_micro, initial, jnp.arange(MICRO, dtype=jnp.int32))
    factor = 1.0 / (MICRO * BATCH)
    return (jnp.swapaxes(adjoints, 0, 1), totals[0] * factor, totals[1] * factor, totals[2] * factor, totals[3] * factor, totals[4] * factor)
```

```python
import functools

import jax
import jax.numpy as jnp
from jax import lax
from jax.experimental import pallas as pl
from jax.experimental.pallas import tpu as pltpu
from jax.sharding import PartitionSpec as P

MESH = pl.DeviceIdType.MESH
EPSILON = 1e-06
F32 = jnp.float32
BF16 = jnp.bfloat16
LANES = 128
OFF = 8
CORES = 2
XS = 4
TAPS = 49
BIAS, GAIN, SHIFT, SCALE = 49, 50, 51, 52
SUM_G, SUM_GN, SUM_MIX = 49, 50, 51


def body(
    geometry,
    x_ref,
    adj_ref,
    kern_ref,
    bias_ref,
    gain_ref,
    shift_ref,
    scale_ref,
    out_ref,
    kgrad_ref,
    bgrad_ref,
    ggrad_ref,
    sgrad_ref,
    lgrad_ref,
    stage,
    own,
    gathered,
    by_channel,
    weights,
    xbuf,
    xhalo,
    xpad,
    mixed,
    gbuf,
    gmix,
    ghalo,
    gpad,
    stats,
    kacc,
    terms,
    flat,
    pieces,
    got1,
    sum1,
    got2,
    sum2,
    got3,
    local_sem,
    z_send,
    z_recv,
    x_send,
    x_recv,
    c_send,
    c_recv,
    xh_send,
    xh_recv,
    gh_send,
    gh_recv,
    seg_send,
    seg_recv,
    r1_send,
    r1_recv,
    r2_send,
    r2_recv,
    r3_send,
    r3_recv,
):
    zs, xs_count, rows, cpd, chunks, height, width = geometry
    xcs = xs_count * CORES
    channels = chunks * LANES
    seg = lax.axis_index("segment")
    dp = lax.axis_index("dp")
    row = lax.axis_index("rows")
    z = dp // xcs
    xc = dp % xcs
    x = xc // CORES
    core = xc % CORES
    zz = z % rows

    def dp_of(z_at, xc_at):
        return z_at * xcs + xc_at

    def remote(src, dst, send, recv, **where):
        return pltpu.make_async_remote_copy(
            src_ref=src, dst_ref=dst, send_sem=send, recv_sem=recv, device_id=where, device_id_type=MESH
        )

    barrier = pltpu.get_barrier_semaphore()

    def greet(**where):
        pl.semaphore_signal(barrier, inc=1, device_id=where, device_id_type=MESH)

    def own_x(m):
        return pltpu.make_async_copy(x_ref.at[m], xbuf.at[m], local_sem.at[m])

    def own_adj(m):
        return pltpu.make_async_copy(adj_ref.at[m], gbuf.at[m], local_sem.at[2 + m])

    for m in range(2):
        own_x(m).start()

    for k in range(1, zs):
        greet(dp=dp_of((z + k) % zs, xc))
    for k in range(1, xcs):
        greet(dp=dp_of(z, (xc + k) % xcs))
    for k in range(1, rows):
        greet(rows=(row + k) % rows)
    greet(segment=1 - seg)
    for k in range(zs):
        if k == 0:

            @pl.when(row != zz)
            def _():
                greet(rows=zz)
        else:
            greet(dp=dp_of((z + k) % zs, xc), rows=zz)

    stage[...] = jnp.zeros_like(stage)
    stage[BIAS : BIAS + 1, 0:cpd] = bias_ref[...].astype(F32)
    stage[GAIN : GAIN + 1, 0:cpd] = gain_ref[...].astype(F32)
    stage[SHIFT : SHIFT + 1, 0:cpd] = shift_ref[...].astype(F32)
    stage[SCALE : SCALE + 1, 0:cpd] = scale_ref[...].astype(F32)
    vectors = jnp.transpose(stage[...])[0:32]
    own[...] = jnp.zeros_like(own)
    own[0:cpd, 0:TAPS] = kern_ref[...].astype(F32)
    gathered[z, x, core] = (vectors + own[...]).astype(BF16)

    known = (zs - 1) + (xcs - 1) + (rows - 1) + 1 + zs

    @pl.when(row != zz)
    def _():
        pl.semaphore_wait(barrier, known)

    @pl.when(row == zz)
    def _():
        pl.semaphore_wait(barrier, known - 1)

    def z_copy(k):
        return remote(
            gathered.at[z, x, core],
            gathered.at[z, x, core],
            z_send.at[k - 1],
            z_recv.at[z],
            dp=dp_of((z + k) % zs, xc),
        )

    def z_arrival(k):
        src = (z + k) % zs
        return remote(
            gathered.at[src, x, core], gathered.at[src, x, core], z_send.at[k - 1], z_recv.at[src], dp=dp_of(src, xc)
        )

    def x_copy(k):
        return remote(
            gathered.at[:, x, core],
            gathered.at[:, x, core],
            x_send.at[k - 1],
            x_recv.at[x],
            dp=dp_of(z, ((x + k) % xs_count) * CORES + core),
        )

    def x_arrival(k):
        src = (x + k) % xs_count
        return remote(
            gathered.at[:, src, core],
            gathered.at[:, src, core],
            x_send.at[k - 1],
            x_recv.at[src],
            dp=dp_of(z, src * CORES + core),
        )

    def c_copy(k):
        src = (x + k) % xs_count
        return remote(
            gathered.at[:, src, core],
            gathered.at[:, src, core],
            c_send.at[k],
            c_recv.at[src],
            dp=dp_of(z, x * CORES + 1 - core),
        )

    def c_arrival(k):
        src = (x + k) % xs_count
        return remote(
            gathered.at[:, src, 1 - core],
            gathered.at[:, src, 1 - core],
            c_send.at[k],
            c_recv.at[src],
            dp=dp_of(z, x * CORES + 1 - core),
        )

    for k in range(1, zs):
        z_copy(k).start()

    def x_down(m):
        return remote(x_ref.at[m, height - 3 : height], xhalo.at[m, 0], xh_send.at[m, 0], xh_recv.at[m, 0], rows=(row + 1) % rows)

    def x_up(m):
        return remote(x_ref.at[m, 0:3], xhalo.at[m, 1], xh_send.at[m, 1], xh_recv.at[m, 1], rows=(row + rows - 1) % rows)

    def g_down(m):
        return remote(gmix.at[m, height - 3 : height], ghalo.at[m, 0], gh_send.at[m, 0], gh_recv.at[m, 0], rows=(row + 1) % rows)

    def g_up(m):
        return remote(gmix.at[m, 0:3], ghalo.at[m, 1], gh_send.at[m, 1], gh_recv.at[m, 1], rows=(row + rows - 1) % rows)

    for m in range(2):

        @pl.when(row < rows - 1)
        def _():
            x_down(m).start()

        @pl.when(row > 0)
        def _():
            x_up(m).start()

    @pl.when(seg == 1)
    def _():
        for m in range(2):
            own_adj(m).start()

    def clear(ch, carry):
        for m in range(2):
            for ref in (xpad, gpad):
                ref[m, ch, :, 0:OFF, :] = jnp.zeros((height + 6, OFF, LANES), F32)
                ref[m, ch, :, OFF + width : 2 * OFF + width, :] = jnp.zeros((height + 6, OFF, LANES), F32)
                ref[m, ch, 0:3, OFF : OFF + width, :] = jnp.zeros((3, width, LANES), F32)
                ref[m, ch, height + 3 : height + 6, OFF : OFF + width, :] = jnp.zeros((3, width, LANES), F32)
        return carry

    lax.fori_loop(0, chunks, clear, 0)

    for m in range(2):
        own_x(m).wait()

    def lanes_of(ch):
        return pl.ds(pl.multiple_of(ch * LANES, LANES), LANES)

    def widen(ch, carry):
        for m in range(2):
            xpad[m, ch, 3 : 3 + height, OFF : OFF + width, :] = xbuf[m, :, :, lanes_of(ch)].astype(F32)
        return carry

    lax.fori_loop(0, chunks, widen, 0)

    for k in range(1, zs):
        z_arrival(k).wait_recv()
    for k in range(1, xs_count):
        x_copy(k).start()
    c_copy(0).start()
    for k in range(1, xs_count):
        x_arrival(k).wait_recv()
        c_copy(k).start()
    for k in range(xs_count):
        c_arrival(k).wait_recv()

    def place(d, carry):
        block = gathered[d // xcs, (d % xcs) // CORES, d % CORES].astype(F32)
        by_channel[pl.ds(pl.multiple_of(d * cpd, 8), cpd), :] = block[0:cpd]
        return carry

    lax.fori_loop(0, zs * xcs, place, 0)

    def turn(ch, carry):
        block = by_channel[pl.ds(pl.multiple_of(ch * LANES, LANES), LANES), :]
        weights[ch] = jnp.transpose(block)[0:64]
        return carry

    lax.fori_loop(0, chunks, turn, 0)

    def put_halo(pad, halo, m, side, start):
        def one(ch, carry):
            pad[m, ch, start : start + 3, OFF : OFF + width, :] = halo[m, side, :, :, lanes_of(ch)].astype(F32)
            return carry

        lax.fori_loop(0, chunks, one, 0)

    def par(ch, which):
        return weights[ch, which : which + 1, :][None]

    inverse_count = 1.0 / channels

    def forward(m, carry):
        @pl.when(row > 0)
        def _():
            x_down(m).wait_recv()
            put_halo(xpad, xhalo, m, 0, 0)

        @pl.when(row < rows - 1)
        def _():
            x_up(m).wait_recv()
            put_halo(xpad, xhalo, m, 1, 3 + height)

        def conv(ch, total):
            acc = jnp.zeros((height, width, LANES), F32) + par(ch, BIAS)
            for c in range(7):
                shifted = xpad[m, ch, :, OFF - 3 + c : OFF - 3 + c + width, :]
                for r in range(7):
                    acc = acc + shifted[r : r + height] * par(ch, 7 * r + c)
            mixed[m, ch] = acc
            return total + acc

        total = lax.fori_loop(0, chunks, conv, jnp.zeros((height, width, LANES), F32))
        mean = jnp.sum(total, axis=-1, keepdims=True) * inverse_count

        def spread(ch, total):
            centred = mixed[m, ch] - mean
            return total + centred * centred

        squares = lax.fori_loop(0, chunks, spread, jnp.zeros((height, width, LANES), F32))
        variance = jnp.sum(squares, axis=-1, keepdims=True) * inverse_count
        inverse = lax.rsqrt(variance + EPSILON)
        stats[m, 0] = jnp.broadcast_to(mean, (height, width, LANES))
        stats[m, 1] = jnp.broadcast_to(inverse, (height, width, LANES))
        return carry

    lax.fori_loop(0, 2, forward, 0)

    def folded(value):
        flat_rows = jnp.sum(value, axis=0)
        total = flat_rows[0:8]
        for at in range(8, width, 8):
            total = total + flat_rows[at : at + 8]
        return total

    def seg_copy(m):
        return remote(out_ref.at[m], gbuf.at[m], seg_send.at[m], seg_recv.at[m], segment=1 - seg)

    def keep(m, ch, which, value):
        @pl.when(m == 0)
        def _():
            kacc[ch, which] = value

        @pl.when(m != 0)
        def _():
            kacc[ch, which] = kacc[ch, which] + value

    def norm_back(m):
        @pl.when(seg == 1)
        def _():
            own_adj(m).wait()

        @pl.when(seg == 0)
        def _():
            seg_copy(m).wait_recv()

        mean = stats[m, 0]
        inverse = stats[m, 1]

        def first(ch, sums):
            normed = (mixed[m, ch] - mean) * inverse
            mixed[m, ch] = normed
            upstream = gbuf[m, :, :, lanes_of(ch)].astype(F32)
            both = upstream * normed
            keep(m, ch, SUM_G, folded(upstream))
            keep(m, ch, SUM_GN, folded(both))
            factor = par(ch, SCALE) * par(ch, GAIN)
            return sums[0] + upstream * factor, sums[1] + both * factor

        zero = jnp.zeros((height, width, LANES), F32)
        plain, weighted = lax.fori_loop(0, chunks, first, (zero, zero))
        plain = jnp.sum(plain, axis=-1, keepdims=True) * inverse_count
        weighted = jnp.sum(weighted, axis=-1, keepdims=True) * inverse_count

        def second(ch, carry):
            upstream = gbuf[m, :, :, lanes_of(ch)].astype(F32)
            factor = par(ch, SCALE) * par(ch, GAIN)
            grad = inverse * (upstream * factor - plain - mixed[m, ch] * weighted)
            rounded = grad.astype(BF16)
            gmix[m, :, :, lanes_of(ch)] = rounded
            again = rounded.astype(F32)
            gpad[m, ch, 3 : 3 + height, OFF : OFF + width, :] = again
            keep(m, ch, SUM_MIX, folded(again))
            return carry

        lax.fori_loop(0, chunks, second, 0)

        @pl.when(row < rows - 1)
        def _():
            g_down(m).start()

        @pl.when(row > 0)
        def _():
            g_up(m).start()

    def adjoint(m):
        @pl.when(row > 0)
        def _():
            g_down(m).wait_recv()
            put_halo(gpad, ghalo, m, 0, 0)

        @pl.when(row < rows - 1)
        def _():
            g_up(m).wait_recv()
            put_halo(gpad, ghalo, m, 1, 3 + height)

        def conv(ch, carry):
            acc = gbuf[m, :, :, lanes_of(ch)].astype(F32)
            for c in range(7):
                shifted = gpad[m, ch, :, OFF + 3 - c : OFF + 3 - c + width, :]
                for r in range(7):
                    acc = acc + shifted[6 - r : 6 - r + height] * par(ch, 7 * r + c)
            out_ref[m, :, :, lanes_of(ch)] = acc.astype(BF16)
            return carry

        lax.fori_loop(0, chunks, conv, 0)

        @pl.when(seg == 1)
        def _():
            seg_copy(m).start()

    def r1_copy(k):
        to = (xc + k) % xcs
        return remote(pieces.at[:, to], got1.at[xc], r1_send.at[k - 1], r1_recv.at[xc], dp=dp_of(z, to))

    def r1_arrival(k):
        src = (xc + k) % xcs
        return remote(pieces.at[:, src], got1.at[src], r1_send.at[k - 1], r1_recv.at[src], dp=dp_of(z, src))

    def taps(m):
        def one(ch, carry):
            grad = gpad[m, ch, 3 : 3 + height, OFF : OFF + width, :]
            for c in range(7):
                shifted = xpad[m, ch, :, OFF - 3 + c : OFF - 3 + c + width, :]
                for r in range(7):
                    keep(m, ch, 7 * r + c, folded(shifted[r : r + height] * grad))
            return carry

        lax.fori_loop(0, chunks, one, 0)

        @pl.when(m == 1)
        def _():
            def total(ch, carry):
                terms[ch] = jnp.zeros((64, LANES), F32)
                for t in range(TAPS + 3):
                    terms[ch, t : t + 1, :] = jnp.sum(kacc[ch, t], axis=0, keepdims=True)
                return carry

            lax.fori_loop(0, chunks, total, 0)
            half = chunks // 2

            def turn_back(ch, carry):
                block = jnp.concatenate([terms[ch], terms[half + ch]], axis=0)
                flat[pl.ds(pl.multiple_of(ch * LANES, LANES), LANES), :] = jnp.transpose(block)
                return carry

            lax.fori_loop(0, half, turn_back, 0)

            def cut(d, carry):
                pieces[d // xcs, d % xcs] = flat[pl.ds(pl.multiple_of(d * cpd, 8), cpd), :]
                return carry

            lax.fori_loop(0, rows * xcs, cut, 0)
            for k in range(1, xcs):
                r1_copy(k).start()

    def step(at, carry):
        m = seg * (at % 2) + (1 - seg) * (at // 3)
        is_norm = seg * (at // 2) + (1 - seg) * (at % 3)
        is_taps = seg * (at // 4) + (1 - seg) * (at % 3 % 2)
        is_adj = seg * (at // 2 % 2) + (1 - seg) * (at % 3 // 2)

        @pl.when(is_norm == 0)
        def _():
            norm_back(m)

        @pl.when(is_taps == 1)
        def _():
            taps(m)

        @pl.when(is_adj == 1)
        def _():
            adjoint(m)

        return carry

    lax.fori_loop(0, 6, step, 0)

    for k in range(1, xcs):
        r1_arrival(k).wait_recv()
    got1[xc] = pieces[:, xc]
    acc = got1[0]
    for k in range(1, xcs):
        acc = acc + got1[k]
    sum1[...] = acc

    def r2_copy(k):
        to = (row + k) % rows
        return remote(sum1.at[to], got2.at[row], r2_send.at[k - 1], r2_recv.at[row], rows=to)

    def r2_arrival(k):
        src = (row + k) % rows
        return remote(sum1.at[src], got2.at[src], r2_send.at[k - 1], r2_recv.at[src], rows=src)

    for k in range(1, rows):
        r2_copy(k).start()
    got2[row] = sum1[row]
    for k in range(1, rows):
        r2_arrival(k).wait_recv()
    acc = got2[0]
    for k in range(1, rows):
        acc = acc + got2[k]
    sum2[...] = acc

    def r3_copy(half, k):
        to_z = half * rows + row
        return remote(sum2, got3.at[z], r3_send.at[half, k], r3_recv.at[z], dp=dp_of(to_z, xc), rows=(row + k) % rows)

    def r3_arrival(k):
        src = (z + k) % zs
        return remote(sum2, got3.at[src], r3_send.at[0, 0], r3_recv.at[src], dp=dp_of(src, xc), rows=zz)

    for half in range(2):
        for k in range(rows):
            if k == 0:

                @pl.when(z != half * rows + row)
                def _():
                    r3_copy(half, 0).start()
            else:
                r3_copy(half, k).start()

    @pl.when(row == zz)
    def _():
        got3[z] = sum2[...]

    @pl.when(row != zz)
    def _():
        r3_arrival(0).wait_recv()

    for k in range(1, zs):
        r3_arrival(k).wait_recv()
    acc = got3[0]
    for k in range(1, zs):
        acc = acc + got3[k]
    stage[...] = jnp.zeros_like(stage)
    stage[0:cpd, :] = acc
    turned = jnp.transpose(stage[...])
    upper = (z // rows) == 1
    scale_by = 1.0 / (2 * zs * xcs)
    final = jnp.where(upper, turned[64:128], turned[0:64]) * scale_by
    kgrad_ref[...] = (jnp.where(upper, pltpu.roll(acc, 64, 1), acc) * scale_by)[:, 0:TAPS]
    sum_g = final[SUM_G : SUM_G + 1, 0:cpd]
    sum_gn = final[SUM_GN : SUM_GN + 1, 0:cpd]
    bgrad_ref[...] = final[SUM_MIX : SUM_MIX + 1, 0:cpd]
    own_scale = scale_ref[...].astype(F32)
    ggrad_ref[...] = own_scale * sum_gn
    sgrad_ref[...] = own_scale * sum_g
    lgrad_ref[...] = gain_ref[...].astype(F32) * sum_gn + shift_ref[...].astype(F32) * sum_g

    for k in range(1, zs):
        z_copy(k).wait_send()
    for k in range(1, xs_count):
        x_copy(k).wait_send()
    for k in range(xs_count):
        c_copy(k).wait_send()
    for m in range(2):

        @pl.when(row < rows - 1)
        def _():
            x_down(m).wait_send()
            g_down(m).wait_send()

        @pl.when(row > 0)
        def _():
            x_up(m).wait_send()
            g_up(m).wait_send()

        @pl.when(seg == 1)
        def _():
            seg_copy(m).wait_send()

    for k in range(1, xcs):
        r1_copy(k).wait_send()
    for k in range(1, rows):
        r2_copy(k).wait_send()
    for half in range(2):
        for k in range(rows):
            if k == 0:

                @pl.when(z != half * rows + row)
                def _():
                    r3_copy(half, 0).wait_send()
            else:
                r3_copy(half, k).wait_send()


def local(xs_count, section_input, adjoint_in, kernel, conv_bias, ln_gain, ln_shift, layer_scale):
    _, micros, images, height, width, channels = section_input.shape
    cpd = kernel.shape[3]
    rows = lax.axis_size("rows")
    zs = lax.axis_size("dp") // (xs_count * CORES)
    xcs = xs_count * CORES
    chunks = channels // LANES
    vmem = pl.BlockSpec(memory_space=pltpu.VMEM)
    hbm = pl.BlockSpec(memory_space=pl.ANY)
    vec = jax.ShapeDtypeStruct((1, cpd), F32)
    dma = pltpu.SemaphoreType.DMA
    scratch = [
        pltpu.VMEM((LANES, LANES), F32),
        pltpu.VMEM((32, LANES), F32),
        pltpu.VMEM((zs, xs_count, CORES, 32, LANES), BF16),
        pltpu.VMEM((channels, LANES), F32),
        pltpu.VMEM((chunks, 64, LANES), F32),
        pltpu.VMEM((2, height, width, channels), BF16),
        pltpu.VMEM((2, 2, 3, width, channels), BF16),
        pltpu.VMEM((2, chunks, height + 6, width + 2 * OFF, LANES), F32),
        pltpu.VMEM((2, chunks, height, width, LANES), F32),
        pltpu.VMEM((2, height, width, channels), BF16),
        pltpu.VMEM((2, height, width, channels), BF16),
        pltpu.VMEM((2, 2, 3, width, channels), BF16),
        pltpu.VMEM((2, chunks, height + 6, width + 2 * OFF, LANES), F32),
        pltpu.VMEM((2, 2, height, width, LANES), F32),
        pltpu.VMEM((chunks, TAPS + 3, 8, LANES), F32),
        pltpu.VMEM((chunks, 64, LANES), F32),
        pltpu.VMEM((channels // 2, LANES), F32),
        pltpu.VMEM((rows, xcs, cpd, LANES), F32),
        pltpu.VMEM((xcs, rows, cpd, LANES), F32),
        pltpu.VMEM((rows, cpd, LANES), F32),
        pltpu.VMEM((rows, cpd, LANES), F32),
        pltpu.VMEM((cpd, LANES), F32),
        pltpu.VMEM((zs, cpd, LANES), F32),
        dma((4,)),
        dma((zs,)),
        dma((zs,)),
        dma((xs_count,)),
        dma((xs_count,)),
        dma((xs_count,)),
        dma((xs_count,)),
        dma((2, 2)),
        dma((2, 2)),
        dma((2, 2)),
        dma((2, 2)),
        dma((2,)),
        dma((2,)),
        dma((xcs,)),
        dma((xcs,)),
        dma((rows,)),
        dma((rows,)),
        dma((2, rows)),
        dma((zs,)),
    ]
    found = pl.pallas_call(
        functools.partial(body, (zs, xs_count, rows, cpd, chunks, height, width)),
        out_shape=(
            jax.ShapeDtypeStruct((micros, height, width, channels), BF16),
            jax.ShapeDtypeStruct((cpd, TAPS), F32),
            vec,
            vec,
            vec,
            vec,
        ),
        in_specs=[hbm, hbm] + [vmem] * 5,
        out_specs=(vmem,) * 6,
        scratch_shapes=scratch,
        compiler_params=pltpu.CompilerParams(
            collective_id=0, has_side_effects=True, vmem_limit_bytes=48 * 1024 * 1024
        ),
    )(
        section_input.reshape(micros, height, width, channels),
        adjoint_in.reshape(micros, height, width, channels),
        kernel.reshape(TAPS, cpd).T,
        conv_bias.reshape(1, cpd),
        ln_gain.reshape(1, cpd),
        ln_shift.reshape(1, cpd),
        layer_scale.reshape(1, cpd),
    )
    adjoint, kgrad, bgrad, ggrad, sgrad, lgrad = found
    return (
        adjoint.reshape(section_input.shape),
        kgrad.T.reshape(kernel.shape),
        bgrad.reshape(conv_bias.shape),
        ggrad.reshape(conv_bias.shape),
        sgrad.reshape(conv_bias.shape),
        lgrad.reshape(conv_bias.shape),
    )


def solution(mesh, xs_count=XS):
    placed = (
        P("segment", None, "dp", "rows", None, None),
        P(None, "dp", "rows", None, None),
        P("segment", None, None, "dp"),
        P("segment", None, "dp"),
        P("segment", None, "dp"),
        P("segment", None, "dp"),
        P("segment", None, "dp"),
    )
    return jax.shard_map(
        functools.partial(local, xs_count),
        mesh=mesh,
        in_specs=placed,
        out_specs=(placed[0],) + (placed[2],) + (placed[3],) * 4,
        check_vma=False,
    )
```

```python
import functools

import jax
import jax.numpy as jnp
from jax import lax
from jax.experimental import pallas as pl
from jax.experimental.pallas import tpu as pltpu
from jax.sharding import PartitionSpec as P

MESH = pl.DeviceIdType.MESH
EPSILON = 1e-06
F32 = jnp.float32
BF16 = jnp.bfloat16
LANES = 128
OFF = 8
CORES = 2
XS = 4
TAPS = 49
BIAS, GAIN, SHIFT, SCALE = 49, 50, 51, 52
SUM_G, SUM_GN, SUM_MIX = 49, 50, 51


def body(
    geometry,
    x_ref,
    adj_ref,
    kern_ref,
    bias_ref,
    gain_ref,
    shift_ref,
    scale_ref,
    out_ref,
    kgrad_ref,
    bgrad_ref,
    ggrad_ref,
    sgrad_ref,
    lgrad_ref,
    stage,
    own,
    mine,
    theirs,
    gathered,
    by_channel,
    weights,
    xbuf,
    xhalo,
    xpad,
    mixed,
    gbuf,
    gmix,
    ghalo,
    gpad,
    stats,
    kacc,
    terms,
    flat,
    pieces,
    got1,
    sum1,
    got2,
    sum2,
    got3,
    local_sem,
    p_send,
    p_recv,
    z_send,
    z_recv,
    x_send,
    x_recv,
    c_send,
    c_recv,
    ship_send,
    ship_recv,
    xh_send,
    xh_recv,
    gh_send,
    gh_recv,
    back_send,
    back_recv,
    r1_send,
    r1_recv,
    r2_send,
    r2_recv,
    r3_send,
    r3_recv,
):
    zs, xs_count, rows, cpd, chunks, height, width = geometry
    xcs = xs_count * CORES
    channels = chunks * LANES
    half = lax.axis_index("segment")
    other = 1 - half
    dp = lax.axis_index("dp")
    row = lax.axis_index("rows")
    z = dp // xcs
    xc = dp % xcs
    x = xc // CORES
    core = xc % CORES
    zz = z % rows

    def dp_of(z_at, xc_at):
        return z_at * xcs + xc_at

    def remote(src, dst, send, recv, **where):
        return pltpu.make_async_remote_copy(
            src_ref=src, dst_ref=dst, send_sem=send, recv_sem=recv, device_id=where, device_id_type=MESH
        )

    barrier = pltpu.get_barrier_semaphore()

    def greet(**where):
        pl.semaphore_signal(barrier, inc=1, device_id=where, device_id_type=MESH)

    own_x = pltpu.make_async_copy(x_ref.at[half], xbuf.at[half], local_sem.at[0])
    own_adj = pltpu.make_async_copy(adj_ref.at[half], gbuf.at[1], local_sem.at[1])
    own_x.start()
    own_adj.start()

    for k in range(1, zs):
        greet(dp=dp_of((z + k) % zs, xc))
    for k in range(1, xcs):
        greet(dp=dp_of(z, (xc + k) % xcs))
    for k in range(1, rows):
        greet(rows=(row + k) % rows)
    for k in range(rows):
        greet(segment=other, rows=(row + k) % rows)
    for k in range(zs):
        if k == 0:

            @pl.when(row != zz)
            def _():
                greet(rows=zz)
        else:
            greet(dp=dp_of((z + k) % zs, xc), rows=zz)

    stage[...] = jnp.zeros_like(stage)
    stage[BIAS : BIAS + 1, 0:cpd] = bias_ref[...].astype(F32)
    stage[GAIN : GAIN + 1, 0:cpd] = gain_ref[...].astype(F32)
    stage[SHIFT : SHIFT + 1, 0:cpd] = shift_ref[...].astype(F32)
    stage[SCALE : SCALE + 1, 0:cpd] = scale_ref[...].astype(F32)
    vectors = jnp.transpose(stage[...])[0:32]
    own[...] = jnp.zeros_like(own)
    own[0:cpd, 0:TAPS] = kern_ref[...].astype(F32)
    block = vectors + own[...]
    mine[...] = jnp.where(half == 1, pltpu.roll(block, 64, 1), block).astype(BF16)

    known = (zs - 1) + (xcs - 1) + (rows - 1) + rows + zs

    @pl.when(row != zz)
    def _():
        pl.semaphore_wait(barrier, known)

    @pl.when(row == zz)
    def _():
        pl.semaphore_wait(barrier, known - 1)

    swap = remote(mine, theirs, p_send.at[0], p_recv.at[0], segment=other)
    swap.start()

    ship = remote(x_ref.at[other], xbuf.at[half], ship_send.at[0], ship_recv.at[0], segment=other)
    shipped = remote(x_ref.at[other], xbuf.at[other], ship_send.at[0], ship_recv.at[0], segment=other)
    ship.start()

    def own_down():
        return remote(x_ref.at[half, height - 3 : height], xhalo.at[half, 0], xh_send.at[half, 0], xh_recv.at[half, 0], rows=(row + 1) % rows)

    def own_up():
        return remote(x_ref.at[half, 0:3], xhalo.at[half, 1], xh_send.at[half, 1], xh_recv.at[half, 1], rows=(row + rows - 1) % rows)

    def x_down(s):
        return remote(xbuf.at[s, height - 3 : height], xhalo.at[s, 0], xh_send.at[s, 0], xh_recv.at[s, 0], rows=(row + 1) % rows)

    def x_up(s):
        return remote(xbuf.at[s, 0:3], xhalo.at[s, 1], xh_send.at[s, 1], xh_recv.at[s, 1], rows=(row + rows - 1) % rows)

    def g_down(s):
        return remote(gmix.at[s, height - 3 : height], ghalo.at[s, 0], gh_send.at[s, 0], gh_recv.at[s, 0], rows=(row + 1) % rows)

    def g_up(s):
        return remote(gmix.at[s, 0:3], ghalo.at[s, 1], gh_send.at[s, 1], gh_recv.at[s, 1], rows=(row + rows - 1) % rows)

    @pl.when(row < rows - 1)
    def _():
        own_down().start()

    @pl.when(row > 0)
    def _():
        own_up().start()

    def clear(ch, carry):
        for s in range(2):
            for ref in (xpad, gpad):
                ref[s, ch, :, 0:OFF, :] = jnp.zeros((height + 6, OFF, LANES), F32)
                ref[s, ch, :, OFF + width : 2 * OFF + width, :] = jnp.zeros((height + 6, OFF, LANES), F32)
                ref[s, ch, 0:3, OFF : OFF + width, :] = jnp.zeros((3, width, LANES), F32)
                ref[s, ch, height + 3 : height + 6, OFF : OFF + width, :] = jnp.zeros((3, width, LANES), F32)
        return carry

    def lanes_of(ch):
        return pl.ds(pl.multiple_of(ch * LANES, LANES), LANES)

    def widen(s):
        def one(ch, carry):
            xpad[s, ch, 3 : 3 + height, OFF : OFF + width, :] = xbuf[s, :, :, lanes_of(ch)].astype(F32)
            return carry

        lax.fori_loop(0, chunks, one, 0)

    def z_copy(k):
        return remote(
            gathered.at[z, x, core],
            gathered.at[z, x, core],
            z_send.at[k - 1],
            z_recv.at[z],
            dp=dp_of((z + k) % zs, xc),
        )

    def z_arrival(k):
        src = (z + k) % zs
        return remote(
            gathered.at[src, x, core], gathered.at[src, x, core], z_send.at[k - 1], z_recv.at[src], dp=dp_of(src, xc)
        )

    def x_copy(k):
        return remote(
            gathered.at[:, x, core],
            gathered.at[:, x, core],
            x_send.at[k - 1],
            x_recv.at[x],
            dp=dp_of(z, ((x + k) % xs_count) * CORES + core),
        )

    def x_arrival(k):
        src = (x + k) % xs_count
        return remote(
            gathered.at[:, src, core],
            gathered.at[:, src, core],
            x_send.at[k - 1],
            x_recv.at[src],
            dp=dp_of(z, src * CORES + core),
        )

    def c_copy(k):
        src = (x + k) % xs_count
        return remote(
            gathered.at[:, src, core],
            gathered.at[:, src, core],
            c_send.at[k],
            c_recv.at[src],
            dp=dp_of(z, x * CORES + 1 - core),
        )

    def c_arrival(k):
        src = (x + k) % xs_count
        return remote(
            gathered.at[:, src, 1 - core],
            gathered.at[:, src, 1 - core],
            c_send.at[k],
            c_recv.at[src],
            dp=dp_of(z, x * CORES + 1 - core),
        )

    swap.wait_recv()
    gathered[z, x, core] = (mine[...].astype(F32) + theirs[...].astype(F32)).astype(BF16)
    for k in range(1, zs):
        z_copy(k).start()
    lax.fori_loop(0, chunks, clear, 0)
    for k in range(1, zs):
        z_arrival(k).wait_recv()
    for k in range(1, xs_count):
        x_copy(k).start()
    c_copy(0).start()
    own_x.wait()
    widen(half)
    for k in range(1, xs_count):
        x_arrival(k).wait_recv()
        c_copy(k).start()
    for k in range(xs_count):
        c_arrival(k).wait_recv()

    def place(d, carry):
        got = gathered[d // xcs, (d % xcs) // CORES, d % CORES].astype(F32)
        by_channel[pl.ds(pl.multiple_of(d * cpd, 8), cpd), :] = got[0:cpd]
        return carry

    lax.fori_loop(0, zs * xcs, place, 0)

    def turn(ch, carry):
        turned = jnp.transpose(by_channel[pl.ds(pl.multiple_of(ch * LANES, LANES), LANES), :])
        weights[0, ch] = turned[0:64]
        weights[1, ch] = turned[64:128]
        return carry

    lax.fori_loop(0, chunks, turn, 0)

    def put_halo(pad, halo, s, side, start):
        def one(ch, carry):
            pad[s, ch, start : start + 3, OFF : OFF + width, :] = halo[s, side, :, :, lanes_of(ch)].astype(F32)
            return carry

        lax.fori_loop(0, chunks, one, 0)

    def par(s, ch, which):
        return weights[s, ch, which : which + 1, :][None]

    inverse_count = 1.0 / channels

    def arrive(s):
        shipped.wait_recv()

        @pl.when(row < rows - 1)
        def _():
            x_down(s).start()

        @pl.when(row > 0)
        def _():
            x_up(s).start()

        widen(s)

    def forward(s):
        @pl.when(row > 0)
        def _():
            x_down(s).wait_recv()
            put_halo(xpad, xhalo, s, 0, 0)

        @pl.when(row < rows - 1)
        def _():
            x_up(s).wait_recv()
            put_halo(xpad, xhalo, s, 1, 3 + height)

        def conv(ch, total):
            acc = jnp.zeros((height, width, LANES), F32) + par(s, ch, BIAS)
            for c in range(7):
                shifted = xpad[s, ch, :, OFF - 3 + c : OFF - 3 + c + width, :]
                for r in range(7):
                    acc = acc + shifted[r : r + height] * par(s, ch, 7 * r + c)
            mixed[s, ch] = acc
            return total + acc

        total = lax.fori_loop(0, chunks, conv, jnp.zeros((height, width, LANES), F32))
        mean = jnp.sum(total, axis=-1, keepdims=True) * inverse_count
        stats[s, 0] = jnp.broadcast_to(mean, (height, width, LANES))
        mean = stats[s, 0]

        def spread(ch, total):
            centred = mixed[s, ch] - mean
            return total + centred * centred

        squares = lax.fori_loop(0, chunks, spread, jnp.zeros((height, width, LANES), F32))
        variance = jnp.sum(squares, axis=-1, keepdims=True) * inverse_count
        inverse = lax.rsqrt(variance + EPSILON)
        stats[s, 1] = jnp.broadcast_to(inverse, (height, width, LANES))

    def folded(value):
        flat_rows = jnp.sum(value, axis=0)
        total = flat_rows[0:8]
        for at in range(8, width, 8):
            total = total + flat_rows[at : at + 8]
        return total

    def norm_back(s):
        @pl.when(s == 1)
        def _():
            own_adj.wait()

        mean = stats[s, 0]
        inverse = stats[s, 1]

        def first(ch, sums):
            normed = (mixed[s, ch] - mean) * inverse
            mixed[s, ch] = normed
            upstream = gbuf[s, :, :, lanes_of(ch)].astype(F32)
            both = upstream * normed
            kacc[ch, SUM_G] = folded(upstream)
            kacc[ch, SUM_GN] = folded(both)
            factor = par(s, ch, SCALE) * par(s, ch, GAIN)
            return sums[0] + upstream * factor, sums[1] + both * factor

        zero = jnp.zeros((height, width, LANES), F32)
        plain, weighted = lax.fori_loop(0, chunks, first, (zero, zero))
        plain = jnp.sum(plain, axis=-1, keepdims=True) * inverse_count
        weighted = jnp.sum(weighted, axis=-1, keepdims=True) * inverse_count

        def second(ch, carry):
            upstream = gbuf[s, :, :, lanes_of(ch)].astype(F32)
            factor = par(s, ch, SCALE) * par(s, ch, GAIN)
            grad = inverse * (upstream * factor - plain - mixed[s, ch] * weighted)
            rounded = grad.astype(BF16)
            gmix[s, :, :, lanes_of(ch)] = rounded
            again = rounded.astype(F32)
            gpad[s, ch, 3 : 3 + height, OFF : OFF + width, :] = again
            kacc[ch, SUM_MIX] = folded(again)
            return carry

        lax.fori_loop(0, chunks, second, 0)

        @pl.when(row < rows - 1)
        def _():
            g_down(s).start()

        @pl.when(row > 0)
        def _():
            g_up(s).start()

    def keep_out(s):
        return pltpu.make_async_copy(gbuf.at[1 - s], out_ref.at[half], local_sem.at[2])

    def send_out(s):
        return remote(gbuf.at[1 - s], out_ref.at[half], back_send.at[0], back_recv.at[0], segment=other)

    def out_arrival():
        return remote(gbuf.at[0], out_ref.at[other], back_send.at[0], back_recv.at[0], segment=other)

    def adjoint(s):
        @pl.when(row > 0)
        def _():
            g_down(s).wait_recv()
            put_halo(gpad, ghalo, s, 0, 0)

        @pl.when(row < rows - 1)
        def _():
            g_up(s).wait_recv()
            put_halo(gpad, ghalo, s, 1, 3 + height)

        def conv(ch, carry):
            acc = gbuf[s, :, :, lanes_of(ch)].astype(F32)
            for c in range(7):
                shifted = gpad[s, ch, :, OFF + 3 - c : OFF + 3 - c + width, :]
                for r in range(7):
                    acc = acc + shifted[6 - r : 6 - r + height] * par(s, ch, 7 * r + c)
            gbuf[1 - s, :, :, lanes_of(ch)] = acc.astype(BF16)
            return carry

        lax.fori_loop(0, chunks, conv, 0)

        @pl.when(s == half)
        def _():
            keep_out(s).start()

        @pl.when(s != half)
        def _():
            send_out(s).start()

    def r1_copy(s, k):
        to = (xc + k) % xcs
        return remote(pieces.at[s, :, to], got1.at[s, xc], r1_send.at[s, k - 1], r1_recv.at[s, xc], dp=dp_of(z, to))

    def r1_arrival(s, k):
        src = (xc + k) % xcs
        return remote(pieces.at[s, :, src], got1.at[s, src], r1_send.at[s, k - 1], r1_recv.at[s, src], dp=dp_of(z, src))

    def taps(s):
        def one(ch, carry):
            grad = gpad[s, ch, 3 : 3 + height, OFF : OFF + width, :]
            for c in range(7):
                shifted = xpad[s, ch, :, OFF - 3 + c : OFF - 3 + c + width, :]
                for r in range(7):
                    kacc[ch, 7 * r + c] = folded(shifted[r : r + height] * grad)
            return carry

        lax.fori_loop(0, chunks, one, 0)

        def total(ch, carry):
            terms[ch] = jnp.zeros((64, LANES), F32)
            for t in range(TAPS + 3):
                terms[ch, t : t + 1, :] = jnp.sum(kacc[ch, t], axis=0, keepdims=True)
            return carry

        lax.fori_loop(0, chunks, total, 0)
        middle = chunks // 2

        def turn_back(ch, carry):
            joined = jnp.concatenate([terms[ch], terms[middle + ch]], axis=0)
            flat[pl.ds(pl.multiple_of(ch * LANES, LANES), LANES), :] = jnp.transpose(joined)
            return carry

        lax.fori_loop(0, middle, turn_back, 0)

        def cut(d, carry):
            pieces[s, d // xcs, d % xcs] = flat[pl.ds(pl.multiple_of(d * cpd, 8), cpd), :]
            return carry

        lax.fori_loop(0, rows * xcs, cut, 0)
        for k in range(1, xcs):
            r1_copy(s, k).start()

    ARRIVE, FORWARD, NORM, TAPS_OF, ADJOINT = range(5)
    lower = ((ARRIVE, 1), (FORWARD, 0), (FORWARD, 1), (NORM, 1), (TAPS_OF, 1), (ADJOINT, 1), (NORM, 0), (TAPS_OF, 0), (ADJOINT, 0))
    upper = ((FORWARD, 1), (NORM, 1), (ARRIVE, 0), (TAPS_OF, 1), (FORWARD, 0), (ADJOINT, 1), (NORM, 0), (TAPS_OF, 0), (ADJOINT, 0))

    def digits(order, which, base):
        return sum(entry[which] * base**at for at, entry in enumerate(order))

    kinds = digits(lower, 0, 8) + half * (digits(upper, 0, 8) - digits(lower, 0, 8))
    slots = digits(lower, 1, 2) + half * (digits(upper, 1, 2) - digits(lower, 1, 2))

    def step(at, carry):
        kinds_left, slots_left = carry
        kind = kinds_left % 8
        s = slots_left % 2
        for number, act in ((ARRIVE, arrive), (FORWARD, forward), (NORM, norm_back), (TAPS_OF, taps), (ADJOINT, adjoint)):

            @pl.when(kind == number)
            def _():
                act(s)

        return kinds_left // 8, slots_left // 2

    lax.fori_loop(0, len(lower), step, (kinds, slots))

    def r2_copy(s, k):
        to = (row + k) % rows
        return remote(
            sum1.at[s, to], got2.at[half, row], r2_send.at[s, k], r2_recv.at[half, row], segment=s, rows=to
        )

    def r2_arrival(k, from_half):
        src = (row + k) % rows
        return remote(
            sum1.at[0, src], got2.at[from_half, src], r2_send.at[0, k], r2_recv.at[from_half, src], segment=other, rows=src
        )

    for s in (1, 0):
        for k in range(1, xcs):
            r1_arrival(s, k).wait_recv()
        got1[s, xc] = pieces[s, :, xc]
        acc = got1[s, 0]
        for k in range(1, xcs):
            acc = acc + got1[s, k]
        sum1[s] = acc

        @pl.when(half == s)
        def _():
            got2[half, row] = sum1[s, row]

        @pl.when(half != s)
        def _():
            r2_copy(s, 0).start()

        for k in range(1, rows):
            r2_copy(s, k).start()

    for k in range(rows):
        if k > 0:
            r2_arrival(k, half).wait_recv()
        r2_arrival(k, other).wait_recv()
    acc = got2[0, 0] + got2[1, 0]
    for k in range(1, rows):
        acc = acc + (got2[0, k] + got2[1, k])
    sum2[...] = acc

    def r3_copy(part, k):
        to_z = part * rows + row
        return remote(sum2, got3.at[z], r3_send.at[part, k], r3_recv.at[z], dp=dp_of(to_z, xc), rows=(row + k) % rows)

    def r3_arrival(k):
        src = (z + k) % zs
        return remote(sum2, got3.at[src], r3_send.at[0, 0], r3_recv.at[src], dp=dp_of(src, xc), rows=zz)

    for part in range(2):
        for k in range(rows):
            if k == 0:

                @pl.when(z != part * rows + row)
                def _():
                    r3_copy(part, 0).start()
            else:
                r3_copy(part, k).start()

    @pl.when(row == zz)
    def _():
        got3[z] = sum2[...]

    @pl.when(row != zz)
    def _():
        r3_arrival(0).wait_recv()

    for k in range(1, zs):
        r3_arrival(k).wait_recv()
    acc = got3[0]
    for k in range(1, zs):
        acc = acc + got3[k]
    scale_by = 1.0 / (2 * zs * xcs)
    acc = jnp.where(z // rows == 1, pltpu.roll(acc, 64, 1), acc) * scale_by
    kgrad_ref[...] = acc[:, 0:TAPS]
    stage[...] = jnp.zeros_like(stage)
    stage[0:cpd, :] = acc
    turned = jnp.transpose(stage[...])
    sum_g = turned[SUM_G : SUM_G + 1, 0:cpd]
    sum_gn = turned[SUM_GN : SUM_GN + 1, 0:cpd]
    bgrad_ref[...] = turned[SUM_MIX : SUM_MIX + 1, 0:cpd]
    own_scale = scale_ref[...].astype(F32)
    ggrad_ref[...] = own_scale * sum_gn
    sgrad_ref[...] = own_scale * sum_g
    lgrad_ref[...] = gain_ref[...].astype(F32) * sum_gn + shift_ref[...].astype(F32) * sum_g

    swap.wait_send()
    ship.wait_send()
    for k in range(1, zs):
        z_copy(k).wait_send()
    for k in range(1, xs_count):
        x_copy(k).wait_send()
    for k in range(xs_count):
        c_copy(k).wait_send()
    for s in range(2):

        @pl.when(row < rows - 1)
        def _():
            x_down(s).wait_send()
            g_down(s).wait_send()

        @pl.when(row > 0)
        def _():
            x_up(s).wait_send()
            g_up(s).wait_send()

        for k in range(1, xcs):
            r1_copy(s, k).wait_send()
        for k in range(1, rows):
            r2_copy(s, k).wait_send()

        @pl.when(half != s)
        def _():
            r2_copy(s, 0).wait_send()

    for part in range(2):
        for k in range(rows):
            if k == 0:

                @pl.when(z != part * rows + row)
                def _():
                    r3_copy(part, 0).wait_send()
            else:
                r3_copy(part, k).wait_send()
    keep_out(0).wait()
    send_out(0).wait_send()
    out_arrival().wait_recv()


def local(xs_count, section_input, adjoint_in, kernel, conv_bias, ln_gain, ln_shift, layer_scale):
    _, micros, images, height, width, channels = section_input.shape
    cpd = kernel.shape[3]
    rows = lax.axis_size("rows")
    zs = lax.axis_size("dp") // (xs_count * CORES)
    xcs = xs_count * CORES
    chunks = channels // LANES
    vmem = pl.BlockSpec(memory_space=pltpu.VMEM)
    hbm = pl.BlockSpec(memory_space=pltpu.HBM)
    vec = jax.ShapeDtypeStruct((1, cpd), F32)
    dma = pltpu.SemaphoreType.DMA
    scratch = [
        pltpu.VMEM((LANES, LANES), F32),
        pltpu.VMEM((32, LANES), F32),
        pltpu.VMEM((32, LANES), BF16),
        pltpu.VMEM((32, LANES), BF16),
        pltpu.VMEM((zs, xs_count, CORES, 32, LANES), BF16),
        pltpu.VMEM((channels, LANES), F32),
        pltpu.VMEM((2, chunks, 64, LANES), F32),
        pltpu.VMEM((2, height, width, channels), BF16),
        pltpu.VMEM((2, 2, 3, width, channels), BF16),
        pltpu.VMEM((2, chunks, height + 6, width + 2 * OFF, LANES), F32),
        pltpu.VMEM((2, chunks, height, width, LANES), F32),
        pltpu.VMEM((2, height, width, channels), BF16),
        pltpu.VMEM((2, height, width, channels), BF16),
        pltpu.VMEM((2, 2, 3, width, channels), BF16),
        pltpu.VMEM((2, chunks, height + 6, width + 2 * OFF, LANES), F32),
        pltpu.VMEM((2, 2, height, width, LANES), F32),
        pltpu.VMEM((chunks, TAPS + 3, 8, LANES), F32),
        pltpu.VMEM((chunks, 64, LANES), F32),
        pltpu.VMEM((channels // 2, LANES), F32),
        pltpu.VMEM((2, rows, xcs, cpd, LANES), F32),
        pltpu.VMEM((2, xcs, rows, cpd, LANES), F32),
        pltpu.VMEM((2, rows, cpd, LANES), F32),
        pltpu.VMEM((2, rows, cpd, LANES), F32),
        pltpu.VMEM((cpd, LANES), F32),
        pltpu.VMEM((zs, cpd, LANES), F32),
        dma((3,)),
        dma((1,)),
        dma((1,)),
        dma((zs,)),
        dma((zs,)),
        dma((xs_count,)),
        dma((xs_count,)),
        dma((xs_count,)),
        dma((xs_count,)),
        dma((1,)),
        dma((1,)),
        dma((2, 2)),
        dma((2, 2)),
        dma((2, 2)),
        dma((2, 2)),
        dma((1,)),
        dma((1,)),
        dma((2, xcs)),
        dma((2, xcs)),
        dma((2, rows)),
        dma((2, rows)),
        dma((2, rows)),
        dma((zs,)),
    ]
    found = pl.pallas_call(
        functools.partial(body, (zs, xs_count, rows, cpd, chunks, height, width)),
        out_shape=(
            jax.ShapeDtypeStruct((micros, height, width, channels), BF16),
            jax.ShapeDtypeStruct((cpd, TAPS), F32),
            vec,
            vec,
            vec,
            vec,
        ),
        in_specs=[hbm, hbm] + [vmem] * 5,
        out_specs=(vmem,) * 6,
        scratch_shapes=scratch,
        compiler_params=pltpu.CompilerParams(
            collective_id=0, has_side_effects=True, vmem_limit_bytes=48 * 1024 * 1024
        ),
    )(
        section_input.reshape(micros, height, width, channels),
        adjoint_in.reshape(micros, height, width, channels),
        kernel.reshape(TAPS, cpd).T,
        conv_bias.reshape(1, cpd),
        ln_gain.reshape(1, cpd),
        ln_shift.reshape(1, cpd),
        layer_scale.reshape(1, cpd),
    )
    adjoint, kgrad, bgrad, ggrad, sgrad, lgrad = found
    return (
        adjoint.reshape(section_input.shape),
        kgrad.T.reshape(kernel.shape),
        bgrad.reshape(conv_bias.shape),
        ggrad.reshape(conv_bias.shape),
        sgrad.reshape(conv_bias.shape),
        lgrad.reshape(conv_bias.shape),
    )


def solution(mesh, xs_count=XS):
    placed = (
        P("segment", None, "dp", "rows", None, None),
        P(None, "dp", "rows", None, None),
        P("segment", None, None, "dp"),
        P("segment", None, "dp"),
        P("segment", None, "dp"),
        P("segment", None, "dp"),
        P("segment", None, "dp"),
    )
    return jax.shard_map(
        functools.partial(local, xs_count),
        mesh=mesh,
        in_specs=placed,
        out_specs=(placed[0],) + (placed[2],) + (placed[3],) * 4,
        check_vma=False,
    )
```

```python
import functools

import jax
import jax.numpy as jnp
from jax import lax
from jax.experimental import pallas as pl
from jax.experimental.pallas import tpu as pltpu
from jax.sharding import PartitionSpec as P

MESH = pl.DeviceIdType.MESH
EPSILON = 1e-06
F32 = jnp.float32
BF16 = jnp.bfloat16
LANES = 128
OFF = 8
CORES = 2
XS = 4
TAPS = 49
BIAS, GAIN, SHIFT, SCALE = 49, 50, 51, 52
SUM_G, SUM_GN, SUM_MIX = 49, 50, 51


def body(
    geometry,
    x_ref,
    adj_ref,
    kern_ref,
    bias_ref,
    gain_ref,
    shift_ref,
    scale_ref,
    out_ref,
    sums_ref,
    stage,
    own,
    gathered,
    by_channel,
    weights,
    xbuf,
    xhalo,
    xpad,
    mixed,
    gbuf,
    gmix,
    ghalo,
    gpad,
    stats,
    kacc,
    terms,
    flat,
    pieces,
    got1,
    sum1,
    got2,
    sum2,
    got3,
    local_sem,
    p_send,
    p_recv,
    z_send,
    z_recv,
    x_send,
    x_recv,
    c_send,
    c_recv,
    ship_send,
    ship_recv,
    xh_send,
    xh_recv,
    gh_send,
    gh_recv,
    back_send,
    back_recv,
    r1_send,
    r1_recv,
    r2_send,
    r2_recv,
    r3_send,
    r3_recv,
):
    zs, xs_count, rows, cpd, chunks, height, width = geometry
    xcs = xs_count * CORES
    channels = chunks * LANES
    half = lax.axis_index("segment")
    other = 1 - half
    dp = lax.axis_index("dp")
    row = lax.axis_index("rows")
    z = dp // xcs
    xc = dp % xcs
    x = xc // CORES
    core = xc % CORES
    zz = z % rows

    def dp_of(z_at, xc_at):
        return z_at * xcs + xc_at

    def remote(src, dst, send, recv, **where):
        return pltpu.make_async_remote_copy(
            src_ref=src, dst_ref=dst, send_sem=send, recv_sem=recv, device_id=where, device_id_type=MESH
        )

    barrier = pltpu.get_barrier_semaphore()

    def greet(**where):
        pl.semaphore_signal(barrier, inc=1, device_id=where, device_id_type=MESH)

    own_x = pltpu.make_async_copy(x_ref.at[half], xbuf.at[half], local_sem.at[0])
    own_adj = pltpu.make_async_copy(adj_ref.at[half], gbuf.at[1], local_sem.at[1])
    own_x.start()
    own_adj.start()

    for k in range(1, zs):
        greet(dp=dp_of((z + k) % zs, xc))
    for k in range(1, xcs):
        greet(dp=dp_of(z, (xc + k) % xcs))
    for k in range(1, rows):
        greet(rows=(row + k) % rows)
    for k in range(rows):
        greet(segment=other, rows=(row + k) % rows)
    for k in range(zs):
        if k == 0:

            @pl.when(row != zz)
            def _():
                greet(rows=zz)
        else:
            greet(dp=dp_of((z + k) % zs, xc), rows=zz)

    stage[...] = jnp.zeros_like(stage)
    stage[BIAS : BIAS + 1, 0:cpd] = bias_ref[...].astype(F32)
    stage[GAIN : GAIN + 1, 0:cpd] = gain_ref[...].astype(F32)
    stage[SHIFT : SHIFT + 1, 0:cpd] = shift_ref[...].astype(F32)
    stage[SCALE : SCALE + 1, 0:cpd] = scale_ref[...].astype(F32)
    vectors = jnp.transpose(stage[...])[0:32]
    own[...] = jnp.zeros_like(own)
    own[0:cpd, 0:TAPS] = kern_ref[...].astype(F32)
    own[...] = own[...] + vectors
    mid = cpd // 2
    gathered[half, z, x, core] = (own[0:16] + pltpu.roll(own[mid : mid + 16], 64, 1)).astype(BF16)

    known = (zs - 1) + (xcs - 1) + (rows - 1) + rows + zs

    @pl.when(row != zz)
    def _():
        pl.semaphore_wait(barrier, known)

    @pl.when(row == zz)
    def _():
        pl.semaphore_wait(barrier, known - 1)

    mine = gathered.at[half, z, x, core]
    swap = remote(mine, mine, p_send.at[0], p_recv.at[0], segment=other)
    swapped = remote(mine, gathered.at[other, z, x, core], p_send.at[0], p_recv.at[0], segment=other)
    swap.start()

    ship = remote(x_ref.at[other], xbuf.at[half], ship_send.at[0], ship_recv.at[0], segment=other)
    shipped = remote(x_ref.at[other], xbuf.at[other], ship_send.at[0], ship_recv.at[0], segment=other)
    ship.start()

    def own_down():
        return remote(x_ref.at[half, height - 3 : height], xhalo.at[half, 0], xh_send.at[half, 0], xh_recv.at[half, 0], rows=(row + 1) % rows)

    def own_up():
        return remote(x_ref.at[half, 0:3], xhalo.at[half, 1], xh_send.at[half, 1], xh_recv.at[half, 1], rows=(row + rows - 1) % rows)

    def x_down(s):
        return remote(xbuf.at[s, height - 3 : height], xhalo.at[s, 0], xh_send.at[s, 0], xh_recv.at[s, 0], rows=(row + 1) % rows)

    def x_up(s):
        return remote(xbuf.at[s, 0:3], xhalo.at[s, 1], xh_send.at[s, 1], xh_recv.at[s, 1], rows=(row + rows - 1) % rows)

    def g_down(s):
        return remote(gmix.at[s, height - 3 : height], ghalo.at[s, 0], gh_send.at[s, 0], gh_recv.at[s, 0], rows=(row + 1) % rows)

    def g_up(s):
        return remote(gmix.at[s, 0:3], ghalo.at[s, 1], gh_send.at[s, 1], gh_recv.at[s, 1], rows=(row + rows - 1) % rows)

    @pl.when(row < rows - 1)
    def _():
        own_down().start()

    @pl.when(row > 0)
    def _():
        own_up().start()

    def clear(ch, carry):
        for s in range(2):
            for ref in (xpad, gpad):
                ref[s, ch, :, 0:OFF, :] = jnp.zeros((height + 6, OFF, LANES), F32)
                ref[s, ch, :, OFF + width : 2 * OFF + width, :] = jnp.zeros((height + 6, OFF, LANES), F32)
                ref[s, ch, 0:3, OFF : OFF + width, :] = jnp.zeros((3, width, LANES), F32)
                ref[s, ch, height + 3 : height + 6, OFF : OFF + width, :] = jnp.zeros((3, width, LANES), F32)
        return carry

    def lanes_of(ch):
        return pl.ds(pl.multiple_of(ch * LANES, LANES), LANES)

    def widen(s):
        def one(ch, carry):
            xpad[s, ch, 3 : 3 + height, OFF : OFF + width, :] = xbuf[s, :, :, lanes_of(ch)].astype(F32)
            return carry

        lax.fori_loop(0, chunks, one, 0)

    def z_copy(s, k):
        block = gathered.at[s, z, x, core]
        return remote(block, block, z_send.at[s, k - 1], z_recv.at[s, z], dp=dp_of((z + k) % zs, xc))

    def z_arrival(s, k):
        src = (z + k) % zs
        block = gathered.at[s, src, x, core]
        return remote(block, block, z_send.at[s, k - 1], z_recv.at[s, src], dp=dp_of(src, xc))

    def x_copy(s, k):
        to = (x + k) % xs_count
        block = gathered.at[s, :, x, core]
        return remote(block, block, x_send.at[s, k - 1], x_recv.at[s, x], dp=dp_of(z, to * CORES + core))

    def x_arrival(s, k):
        src = (x + k) % xs_count
        block = gathered.at[s, :, src, core]
        return remote(block, block, x_send.at[s, k - 1], x_recv.at[s, src], dp=dp_of(z, src * CORES + core))

    def c_copy(s, k):
        src = (x + k) % xs_count
        block = gathered.at[s, :, src, core]
        return remote(block, block, c_send.at[s, k], c_recv.at[s, src], dp=dp_of(z, x * CORES + 1 - core))

    def c_arrival(s, k):
        src = (x + k) % xs_count
        block = gathered.at[s, :, src, 1 - core]
        return remote(block, block, c_send.at[s, k], c_recv.at[s, src], dp=dp_of(z, x * CORES + 1 - core))

    def over_z(s):
        for k in range(1, zs):
            z_copy(s, k).start()

    def over_x(s):
        for k in range(1, zs):
            z_arrival(s, k).wait_recv()
        for k in range(1, xs_count):
            x_copy(s, k).start()
        c_copy(s, 0).start()

    def over_core(s):
        for k in range(1, xs_count):
            x_arrival(s, k).wait_recv()
            c_copy(s, k).start()

    def settle(s):
        for k in range(xs_count):
            c_arrival(s, k).wait_recv()

        def place(at, carry):
            got = gathered[s, at].astype(F32)
            turned = pltpu.roll(got, 64, 3)
            for d in range(xcs):
                by_channel[at, d * cpd : d * cpd + mid, :] = got[d // CORES, d % CORES, 0:mid]
                by_channel[at, d * cpd + mid : (d + 1) * cpd, :] = turned[d // CORES, d % CORES, 0:mid]
            return carry

        lax.fori_loop(0, zs, place, 0)
        span = xcs * cpd
        for ch in range(chunks):
            first, parts = ch * LANES, []
            while first < (ch + 1) * LANES:
                last = min((first // span + 1) * span, (ch + 1) * LANES)
                parts.append(by_channel[first // span, first % span : first % span + last - first, :])
                first = last
            weights[s, ch] = jnp.transpose(jnp.concatenate(parts, axis=0) if len(parts) > 1 else parts[0])[0:64]

    over_z(half)
    lax.fori_loop(0, chunks, clear, 0)
    over_x(half)
    own_x.wait()
    widen(half)
    over_core(half)
    swapped.wait_recv()
    over_z(other)
    settle(half)

    def put_halo(pad, halo, s, side, start):
        def one(ch, carry):
            pad[s, ch, start : start + 3, OFF : OFF + width, :] = halo[s, side, :, :, lanes_of(ch)].astype(F32)
            return carry

        lax.fori_loop(0, chunks, one, 0)

    def par(s, ch, which):
        return weights[s, ch, which : which + 1, :][None]

    inverse_count = 1.0 / channels

    def arrive(s):
        shipped.wait_recv()

        @pl.when(row < rows - 1)
        def _():
            x_down(s).start()

        @pl.when(row > 0)
        def _():
            x_up(s).start()

        widen(s)

    def forward(s):
        @pl.when(row > 0)
        def _():
            x_down(s).wait_recv()
            put_halo(xpad, xhalo, s, 0, 0)

        @pl.when(row < rows - 1)
        def _():
            x_up(s).wait_recv()
            put_halo(xpad, xhalo, s, 1, 3 + height)

        def conv(ch, total):
            acc = jnp.zeros((height, width, LANES), F32) + par(s, ch, BIAS)
            for c in range(7):
                shifted = xpad[s, ch, :, OFF - 3 + c : OFF - 3 + c + width, :]
                for r in range(7):
                    acc = acc + shifted[r : r + height] * par(s, ch, 7 * r + c)
            mixed[s, ch] = acc
            return total + acc

        total = lax.fori_loop(0, chunks, conv, jnp.zeros((height, width, LANES), F32))
        mean = jnp.sum(total, axis=-1, keepdims=True) * inverse_count
        stats[s, 0] = jnp.broadcast_to(mean, (height, width, LANES))
        mean = stats[s, 0]

        def spread(ch, total):
            centred = mixed[s, ch] - mean
            return total + centred * centred

        squares = lax.fori_loop(0, chunks, spread, jnp.zeros((height, width, LANES), F32))
        variance = jnp.sum(squares, axis=-1, keepdims=True) * inverse_count
        inverse = lax.rsqrt(variance + EPSILON)
        stats[s, 1] = jnp.broadcast_to(inverse, (height, width, LANES))

        @pl.when(s == half)
        def _():
            over_x(other)

    def folded(value):
        flat_rows = jnp.sum(value, axis=0)
        total = flat_rows[0:8]
        for at in range(8, width, 8):
            total = total + flat_rows[at : at + 8]
        return total

    def norm_back(s):
        @pl.when(s == 1)
        def _():
            own_adj.wait()

        mean = stats[s, 0]
        inverse = stats[s, 1]

        def first(ch, sums):
            normed = (mixed[s, ch] - mean) * inverse
            mixed[s, ch] = normed
            upstream = gbuf[s, :, :, lanes_of(ch)].astype(F32)
            both = upstream * normed
            kacc[ch, SUM_G] = folded(upstream)
            kacc[ch, SUM_GN] = folded(both)
            factor = par(s, ch, SCALE) * par(s, ch, GAIN)
            return sums[0] + upstream * factor, sums[1] + both * factor

        zero = jnp.zeros((height, width, LANES), F32)
        plain, weighted = lax.fori_loop(0, chunks, first, (zero, zero))
        plain = jnp.sum(plain, axis=-1, keepdims=True) * inverse_count
        weighted = jnp.sum(weighted, axis=-1, keepdims=True) * inverse_count

        def second(ch, carry):
            upstream = gbuf[s, :, :, lanes_of(ch)].astype(F32)
            factor = par(s, ch, SCALE) * par(s, ch, GAIN)
            grad = inverse * (upstream * factor - plain - mixed[s, ch] * weighted)
            rounded = grad.astype(BF16)
            gmix[s, :, :, lanes_of(ch)] = rounded
            again = rounded.astype(F32)
            gpad[s, ch, 3 : 3 + height, OFF : OFF + width, :] = again
            kacc[ch, SUM_MIX] = folded(again)
            return carry

        lax.fori_loop(0, chunks, second, 0)

        @pl.when(row < rows - 1)
        def _():
            g_down(s).start()

        @pl.when(row > 0)
        def _():
            g_up(s).start()

    def keep_out(s):
        return pltpu.make_async_copy(gbuf.at[1 - s], out_ref.at[half], local_sem.at[2])

    def send_out(s):
        return remote(gbuf.at[1 - s], out_ref.at[half], back_send.at[0], back_recv.at[0], segment=other)

    def out_arrival():
        return remote(gbuf.at[0], out_ref.at[other], back_send.at[0], back_recv.at[0], segment=other)

    def adjoint(s):
        @pl.when(row > 0)
        def _():
            g_down(s).wait_recv()
            put_halo(gpad, ghalo, s, 0, 0)

        @pl.when(row < rows - 1)
        def _():
            g_up(s).wait_recv()
            put_halo(gpad, ghalo, s, 1, 3 + height)

        def conv(ch, carry):
            acc = gbuf[s, :, :, lanes_of(ch)].astype(F32)
            for c in range(7):
                shifted = gpad[s, ch, :, OFF + 3 - c : OFF + 3 - c + width, :]
                for r in range(7):
                    acc = acc + shifted[6 - r : 6 - r + height] * par(s, ch, 7 * r + c)
            gbuf[1 - s, :, :, lanes_of(ch)] = acc.astype(BF16)
            return carry

        lax.fori_loop(0, chunks, conv, 0)

        @pl.when(s == half)
        def _():
            keep_out(s).start()

        @pl.when(s != half)
        def _():
            send_out(s).start()

    def r1_copy(s, k):
        to = (xc + k) % xcs
        return remote(pieces.at[s, :, to], got1.at[s, xc], r1_send.at[s, k - 1], r1_recv.at[s, xc], dp=dp_of(z, to))

    def r1_arrival(s, k):
        src = (xc + k) % xcs
        return remote(pieces.at[s, :, src], got1.at[s, src], r1_send.at[s, k - 1], r1_recv.at[s, src], dp=dp_of(z, src))

    def taps(s):
        def one(ch, carry):
            grad = gpad[s, ch, 3 : 3 + height, OFF : OFF + width, :]
            for c in range(7):
                shifted = xpad[s, ch, :, OFF - 3 + c : OFF - 3 + c + width, :]
                for r in range(7):
                    kacc[ch, 7 * r + c] = folded(shifted[r : r + height] * grad)
            return carry

        lax.fori_loop(0, chunks, one, 0)

        def total(ch, carry):
            terms[ch] = jnp.zeros((64, LANES), F32)
            for t in range(TAPS + 3):
                terms[ch, t : t + 1, :] = jnp.sum(kacc[ch, t], axis=0, keepdims=True)
            return carry

        lax.fori_loop(0, chunks, total, 0)
        middle = chunks // 2

        for ch in range(middle):
            joined = jnp.concatenate([terms[ch], terms[middle + ch]], axis=0)
            flat[ch * LANES : (ch + 1) * LANES, :] = jnp.transpose(joined)
        for d in range(rows * xcs):
            pieces[s, d // xcs, d % xcs] = flat[d * cpd : (d + 1) * cpd, :]
        for k in range(1, xcs):
            r1_copy(s, k).start()

    ARRIVE, FORWARD, NORM, TAPS_OF, ADJOINT, OVER_CORE, SETTLE = range(7)
    lower = ((FORWARD, 0), (ARRIVE, 1), (OVER_CORE, 1), (SETTLE, 1), (FORWARD, 1), (NORM, 1), (TAPS_OF, 1))
    upper = ((FORWARD, 1), (NORM, 1), (OVER_CORE, 0), (ARRIVE, 0), (TAPS_OF, 1), (SETTLE, 0), (FORWARD, 0))
    common = ((ADJOINT, 1), (NORM, 0), (TAPS_OF, 0), (ADJOINT, 0))
    acts = (arrive, forward, norm_back, taps, adjoint, over_core, settle)

    def digits(order):
        return sum((2 * kind + s) * 16**at for at, (kind, s) in enumerate(order))

    codes = digits(lower) + half * (digits(upper) - digits(lower))

    def step(at, left):
        code = left % 16
        s = code % 2
        for number, act in enumerate(acts):

            @pl.when(code // 2 == number)
            def _():
                act(s)

        return jnp.where(at == len(lower) - 1, digits(common), left // 16)

    lax.fori_loop(0, len(lower) + len(common), step, codes)

    def r2_copy(s, k):
        to = (row + k) % rows
        return remote(
            sum1.at[s, to], got2.at[half, row], r2_send.at[s, k], r2_recv.at[half, row], segment=s, rows=to
        )

    def r2_arrival(k, from_half):
        src = (row + k) % rows
        return remote(
            sum1.at[0, src], got2.at[from_half, src], r2_send.at[0, k], r2_recv.at[from_half, src], segment=other, rows=src
        )

    for s in (1, 0):
        for k in range(1, xcs):
            r1_arrival(s, k).wait_recv()
        got1[s, xc] = pieces[s, :, xc]
        acc = got1[s, 0]
        for k in range(1, xcs):
            acc = acc + got1[s, k]
        sum1[s] = acc

        @pl.when(half == s)
        def _():
            got2[half, row] = sum1[s, row]

        @pl.when(half != s)
        def _():
            r2_copy(s, 0).start()

        for k in range(1, rows):
            r2_copy(s, k).start()

    for k in range(rows):
        if k > 0:
            r2_arrival(k, half).wait_recv()
        r2_arrival(k, other).wait_recv()
    acc = got2[0, 0] + got2[1, 0]
    for k in range(1, rows):
        acc = acc + (got2[0, k] + got2[1, k])
    sum2[...] = acc

    def r3_copy(part, k):
        to_z = part * rows + row
        return remote(sum2, got3.at[z], r3_send.at[part, k], r3_recv.at[z], dp=dp_of(to_z, xc), rows=(row + k) % rows)

    def r3_arrival(k):
        src = (z + k) % zs
        return remote(sum2, got3.at[src], r3_send.at[0, 0], r3_recv.at[src], dp=dp_of(src, xc), rows=zz)

    for part in range(2):
        for k in range(rows):
            if k == 0:

                @pl.when(z != part * rows + row)
                def _():
                    r3_copy(part, 0).start()
            else:
                r3_copy(part, k).start()

    @pl.when(row == zz)
    def _():
        got3[z] = sum2[...]

    @pl.when(row != zz)
    def _():
        r3_arrival(0).wait_recv()

    for k in range(1, zs):
        r3_arrival(k).wait_recv()
    acc = got3[0]
    for k in range(1, zs):
        acc = acc + got3[k]
    scale_by = 1.0 / (2 * zs * xcs)
    sums_ref[...] = jnp.where(z // rows == 1, pltpu.roll(acc, 64, 1), acc) * scale_by

    swap.wait_send()
    ship.wait_send()
    for s in range(2):
        for k in range(1, zs):
            z_copy(s, k).wait_send()
        for k in range(1, xs_count):
            x_copy(s, k).wait_send()
        for k in range(xs_count):
            c_copy(s, k).wait_send()

        @pl.when(row < rows - 1)
        def _():
            x_down(s).wait_send()
            g_down(s).wait_send()

        @pl.when(row > 0)
        def _():
            x_up(s).wait_send()
            g_up(s).wait_send()

        for k in range(1, xcs):
            r1_copy(s, k).wait_send()
        for k in range(1, rows):
            r2_copy(s, k).wait_send()

        @pl.when(half != s)
        def _():
            r2_copy(s, 0).wait_send()

    for part in range(2):
        for k in range(rows):
            if k == 0:

                @pl.when(z != part * rows + row)
                def _():
                    r3_copy(part, 0).wait_send()
            else:
                r3_copy(part, k).wait_send()
    keep_out(0).wait()
    send_out(0).wait_send()
    out_arrival().wait_recv()


def finish(whole_ref, sums_ref, gain_ref, shift_ref, scale_ref, out_ref, kgrad_ref, bgrad_ref, ggrad_ref, sgrad_ref, lgrad_ref, held, stage, sem):
    count = held.shape[0]
    fetch = [pltpu.make_async_copy(whole_ref.at[m], held.at[m], sem.at[0, m]) for m in range(count)]
    place = [pltpu.make_async_copy(held.at[m], out_ref.at[m], sem.at[1, m]) for m in range(count)]
    for m in range(count):
        fetch[m].start()
    for m in range(count):
        fetch[m].wait()
        place[m].start()
    cpd = sums_ref.shape[0]
    kgrad_ref[...] = sums_ref[:, 0:TAPS]
    stage[...] = jnp.zeros_like(stage)
    stage[0:cpd, :] = sums_ref[...]
    turned = jnp.transpose(stage[...])
    sum_g = turned[SUM_G : SUM_G + 1, 0:cpd]
    sum_gn = turned[SUM_GN : SUM_GN + 1, 0:cpd]
    bgrad_ref[...] = turned[SUM_MIX : SUM_MIX + 1, 0:cpd]
    own_scale = scale_ref[...].astype(F32)
    ggrad_ref[...] = own_scale * sum_gn
    sgrad_ref[...] = own_scale * sum_g
    lgrad_ref[...] = gain_ref[...].astype(F32) * sum_gn + shift_ref[...].astype(F32) * sum_g
    for m in range(count):
        place[m].wait()


def local(xs_count, section_input, adjoint_in, kernel, conv_bias, ln_gain, ln_shift, layer_scale):
    _, micros, images, height, width, channels = section_input.shape
    cpd = kernel.shape[3]
    rows = lax.axis_size("rows")
    zs = lax.axis_size("dp") // (xs_count * CORES)
    xcs = xs_count * CORES
    chunks = channels // LANES
    vmem = pl.BlockSpec(memory_space=pltpu.VMEM)
    hbm = pl.BlockSpec(memory_space=pltpu.HBM)
    vec = jax.ShapeDtypeStruct((1, cpd), F32)
    dma = pltpu.SemaphoreType.DMA
    scratch = [
        pltpu.VMEM((LANES, LANES), F32),
        pltpu.VMEM((32, LANES), F32),
        pltpu.VMEM((2, zs, xs_count, CORES, 16, LANES), BF16),
        pltpu.VMEM((zs, xcs * cpd, LANES), F32),
        pltpu.VMEM((2, chunks, 64, LANES), F32),
        pltpu.VMEM((2, height, width, channels), BF16),
        pltpu.VMEM((2, 2, 3, width, channels), BF16),
        pltpu.VMEM((2, chunks, height + 6, width + 2 * OFF, LANES), F32),
        pltpu.VMEM((2, chunks, height, width, LANES), F32),
        pltpu.VMEM((2, height, width, channels), BF16),
        pltpu.VMEM((2, height, width, channels), BF16),
        pltpu.VMEM((2, 2, 3, width, channels), BF16),
        pltpu.VMEM((2, chunks, height + 6, width + 2 * OFF, LANES), F32),
        pltpu.VMEM((2, 2, height, width, LANES), F32),
        pltpu.VMEM((chunks, TAPS + 3, 8, LANES), F32),
        pltpu.VMEM((chunks, 64, LANES), F32),
        pltpu.VMEM((channels // 2, LANES), F32),
        pltpu.VMEM((2, rows, xcs, cpd, LANES), F32),
        pltpu.VMEM((2, xcs, rows, cpd, LANES), F32),
        pltpu.VMEM((2, rows, cpd, LANES), F32),
        pltpu.VMEM((2, rows, cpd, LANES), F32),
        pltpu.VMEM((cpd, LANES), F32),
        pltpu.VMEM((zs, cpd, LANES), F32),
        dma((3,)),
        dma((1,)),
        dma((1,)),
        dma((2, zs)),
        dma((2, zs)),
        dma((2, xs_count)),
        dma((2, xs_count)),
        dma((2, xs_count)),
        dma((2, xs_count)),
        dma((1,)),
        dma((1,)),
        dma((2, 2)),
        dma((2, 2)),
        dma((2, 2)),
        dma((2, 2)),
        dma((1,)),
        dma((1,)),
        dma((2, xcs)),
        dma((2, xcs)),
        dma((2, rows)),
        dma((2, rows)),
        dma((2, rows)),
        dma((zs,)),
    ]
    vectors = [vector.reshape(1, cpd) for vector in (conv_bias, ln_gain, ln_shift, layer_scale)]
    whole, sums = pl.pallas_call(
        functools.partial(body, (zs, xs_count, rows, cpd, chunks, height, width)),
        out_shape=(
            jax.ShapeDtypeStruct((micros, height, width, channels), BF16),
            jax.ShapeDtypeStruct((cpd, LANES), F32),
        ),
        in_specs=[hbm, hbm] + [vmem] * 5,
        out_specs=(hbm, vmem),
        scratch_shapes=scratch,
        compiler_params=pltpu.CompilerParams(
            collective_id=0, has_side_effects=True, vmem_limit_bytes=60 * 1024 * 1024
        ),
    )(
        section_input.reshape(micros, height, width, channels),
        adjoint_in.reshape(micros, height, width, channels),
        kernel.reshape(TAPS, cpd).T,
        *vectors,
    )
    adjoint, kgrad, bgrad, ggrad, sgrad, lgrad = pl.pallas_call(
        finish,
        out_shape=(
            jax.ShapeDtypeStruct((micros, height, width, channels), BF16),
            jax.ShapeDtypeStruct((cpd, TAPS), F32),
            vec,
            vec,
            vec,
            vec,
        ),
        in_specs=[hbm] + [vmem] * 4,
        out_specs=(hbm,) + (vmem,) * 5,
        scratch_shapes=[
            pltpu.VMEM((micros, height, width, channels), BF16),
            pltpu.VMEM((LANES, LANES), F32),
            dma((2, micros)),
        ],
        compiler_params=pltpu.CompilerParams(vmem_limit_bytes=60 * 1024 * 1024),
    )(whole, sums, *vectors[1:])
    return (
        adjoint.reshape(section_input.shape),
        kgrad.T.reshape(kernel.shape),
        bgrad.reshape(conv_bias.shape),
        ggrad.reshape(conv_bias.shape),
        sgrad.reshape(conv_bias.shape),
        lgrad.reshape(conv_bias.shape),
    )


def solution(mesh, xs_count=XS):
    placed = (
        P("segment", None, "dp", "rows", None, None),
        P(None, "dp", "rows", None, None),
        P("segment", None, None, "dp"),
        P("segment", None, "dp"),
        P("segment", None, "dp"),
        P("segment", None, "dp"),
        P("segment", None, "dp"),
    )
    return jax.shard_map(
        functools.partial(local, xs_count),
        mesh=mesh,
        in_specs=placed,
        out_specs=(placed[0],) + (placed[2],) + (placed[3],) * 4,
        check_vma=False,
    )
```

```python
import functools

import jax
import jax.numpy as jnp
from jax import lax
from jax.experimental import pallas as pl
from jax.experimental.pallas import tpu as pltpu
from jax.sharding import PartitionSpec as P

MESH = pl.DeviceIdType.MESH
EPSILON = 1e-06
F32 = jnp.float32
BF16 = jnp.bfloat16
LANES = 128
OFF = 8
CORES = 2
XS = 4
TAPS = 49
BIAS, GAIN, SHIFT, SCALE = 49, 50, 51, 52
BLOCKS = 3
SUM_G, SUM_GN, SUM_MIX = 49, 50, 51


def body(
    geometry,
    x_ref,
    adj_ref,
    kern_ref,
    bias_ref,
    gain_ref,
    shift_ref,
    scale_ref,
    out_ref,
    sums_ref,
    stage,
    own,
    gathered,
    by_channel,
    weights,
    xbuf,
    xhalo,
    xpad,
    mixed,
    gbuf,
    gmix,
    ghalo,
    gpad,
    stats,
    kacc,
    terms,
    flat,
    pieces,
    got1,
    sum1,
    got2,
    sum2,
    got3,
    local_sem,
    p_send,
    p_recv,
    z_send,
    z_recv,
    x_send,
    x_recv,
    c_send,
    c_recv,
    ship_send,
    ship_recv,
    xh_send,
    xh_recv,
    gh_send,
    gh_recv,
    back_send,
    back_recv,
    r1_send,
    r1_recv,
    r2_send,
    r2_recv,
    r3_send,
    r3_recv,
):
    zs, xs_count, rows, cpd, chunks, height, width = geometry
    xcs = xs_count * CORES
    channels = chunks * LANES
    half = lax.axis_index("segment")
    other = 1 - half
    dp = lax.axis_index("dp")
    row = lax.axis_index("rows")
    z = dp // xcs
    xc = dp % xcs
    x = xc // CORES
    core = xc % CORES
    zz = z % rows

    def dp_of(z_at, xc_at):
        return z_at * xcs + xc_at

    def remote(src, dst, send, recv, **where):
        return pltpu.make_async_remote_copy(
            src_ref=src, dst_ref=dst, send_sem=send, recv_sem=recv, device_id=where, device_id_type=MESH
        )

    barrier = pltpu.get_barrier_semaphore()

    def greet(**where):
        pl.semaphore_signal(barrier, inc=1, device_id=where, device_id_type=MESH)

    own_x = pltpu.make_async_copy(x_ref.at[half], xbuf.at[half], local_sem.at[0])
    own_adj = pltpu.make_async_copy(adj_ref.at[half], gbuf.at[1], local_sem.at[1])
    own_x.start()
    own_adj.start()

    for k in range(1, zs):
        greet(dp=dp_of((z + k) % zs, xc))
    for k in range(1, xcs):
        greet(dp=dp_of(z, (xc + k) % xcs))
    for k in range(1, rows):
        greet(rows=(row + k) % rows)
    for k in range(rows):
        greet(segment=other, rows=(row + k) % rows)
    for k in range(zs):
        if k == 0:

            @pl.when(row != zz)
            def _():
                greet(rows=zz)
        else:
            greet(dp=dp_of((z + k) % zs, xc), rows=zz)

    stage[...] = jnp.zeros_like(stage)
    stage[BIAS : BIAS + 1, 0:cpd] = bias_ref[...].astype(F32)
    stage[GAIN : GAIN + 1, 0:cpd] = gain_ref[...].astype(F32)
    stage[SHIFT : SHIFT + 1, 0:cpd] = shift_ref[...].astype(F32)
    stage[SCALE : SCALE + 1, 0:cpd] = scale_ref[...].astype(F32)
    vectors = jnp.transpose(stage[...])[0:32]
    own[...] = jnp.zeros_like(own)
    own[0:cpd, 0:TAPS] = kern_ref[...].astype(F32)
    own[...] = own[...] + vectors
    mid = cpd // 2
    gathered[half, z, x, core] = (own[0:16] + pltpu.roll(own[mid : mid + 16], 64, 1)).astype(BF16)

    known = (zs - 1) + (xcs - 1) + (rows - 1) + rows + zs

    @pl.when(row != zz)
    def _():
        pl.semaphore_wait(barrier, known)

    @pl.when(row == zz)
    def _():
        pl.semaphore_wait(barrier, known - 1)

    mine = gathered.at[half, z, x, core]
    swap = remote(mine, mine, p_send.at[0], p_recv.at[0], segment=other)
    swapped = remote(mine, gathered.at[other, z, x, core], p_send.at[0], p_recv.at[0], segment=other)
    swap.start()

    ship = remote(x_ref.at[other], xbuf.at[half], ship_send.at[0], ship_recv.at[0], segment=other)
    shipped = remote(x_ref.at[other], xbuf.at[other], ship_send.at[0], ship_recv.at[0], segment=other)
    ship.start()

    def own_down():
        return remote(x_ref.at[half, height - 3 : height], xhalo.at[half, 0], xh_send.at[half, 0], xh_recv.at[half, 0], rows=(row + 1) % rows)

    def own_up():
        return remote(x_ref.at[half, 0:3], xhalo.at[half, 1], xh_send.at[half, 1], xh_recv.at[half, 1], rows=(row + rows - 1) % rows)

    def x_down(s):
        return remote(xbuf.at[s, height - 3 : height], xhalo.at[s, 0], xh_send.at[s, 0], xh_recv.at[s, 0], rows=(row + 1) % rows)

    def x_up(s):
        return remote(xbuf.at[s, 0:3], xhalo.at[s, 1], xh_send.at[s, 1], xh_recv.at[s, 1], rows=(row + rows - 1) % rows)

    block_chunks = chunks // BLOCKS
    block_lanes = block_chunks * LANES

    def block_of(b):
        return pl.ds(pl.multiple_of(b * block_lanes, LANES), block_lanes)

    def g_down(s, b):
        return remote(
            gmix.at[s, height - 3 : height, :, block_of(b)],
            ghalo.at[s, 0, :, :, block_of(b)],
            gh_send.at[s, 0, b],
            gh_recv.at[s, 0, b],
            rows=(row + 1) % rows,
        )

    def g_up(s, b):
        return remote(
            gmix.at[s, 0:3, :, block_of(b)],
            ghalo.at[s, 1, :, :, block_of(b)],
            gh_send.at[s, 1, b],
            gh_recv.at[s, 1, b],
            rows=(row + rows - 1) % rows,
        )

    @pl.when(row < rows - 1)
    def _():
        own_down().start()

    @pl.when(row > 0)
    def _():
        own_up().start()

    def clear(ch, carry):
        for s in range(2):
            for ref in (xpad, gpad):
                ref[s, ch, :, 0:OFF, :] = jnp.zeros((height + 6, OFF, LANES), F32)
                ref[s, ch, :, OFF + width : 2 * OFF + width, :] = jnp.zeros((height + 6, OFF, LANES), F32)
                ref[s, ch, 0:3, OFF : OFF + width, :] = jnp.zeros((3, width, LANES), F32)
                ref[s, ch, height + 3 : height + 6, OFF : OFF + width, :] = jnp.zeros((3, width, LANES), F32)
        return carry

    def lanes_of(ch):
        return pl.ds(pl.multiple_of(ch * LANES, LANES), LANES)

    def widen(s):
        def one(ch, carry):
            xpad[s, ch, 3 : 3 + height, OFF : OFF + width, :] = xbuf[s, :, :, lanes_of(ch)].astype(F32)
            return carry

        lax.fori_loop(0, chunks, one, 0)

    def z_copy(s, k):
        block = gathered.at[s, z, x, core]
        return remote(block, block, z_send.at[s, k - 1], z_recv.at[s, z], dp=dp_of((z + k) % zs, xc))

    def z_arrival(s, k):
        src = (z + k) % zs
        block = gathered.at[s, src, x, core]
        return remote(block, block, z_send.at[s, k - 1], z_recv.at[s, src], dp=dp_of(src, xc))

    def x_copy(s, k):
        to = (x + k) % xs_count
        block = gathered.at[s, :, x, core]
        return remote(block, block, x_send.at[s, k - 1], x_recv.at[s, x], dp=dp_of(z, to * CORES + core))

    def x_arrival(s, k):
        src = (x + k) % xs_count
        block = gathered.at[s, :, src, core]
        return remote(block, block, x_send.at[s, k - 1], x_recv.at[s, src], dp=dp_of(z, src * CORES + core))

    def c_copy(s, k):
        src = (x + k) % xs_count
        block = gathered.at[s, :, src, core]
        return remote(block, block, c_send.at[s, k], c_recv.at[s, src], dp=dp_of(z, x * CORES + 1 - core))

    def c_arrival(s, k):
        src = (x + k) % xs_count
        block = gathered.at[s, :, src, 1 - core]
        return remote(block, block, c_send.at[s, k], c_recv.at[s, src], dp=dp_of(z, x * CORES + 1 - core))

    def over_z(s):
        for k in range(1, zs):
            z_copy(s, k).start()

    def over_x(s):
        for k in range(1, zs):
            z_arrival(s, k).wait_recv()
        for k in range(1, xs_count):
            x_copy(s, k).start()
        c_copy(s, 0).start()

    def over_core(s):
        for k in range(1, xs_count):
            x_arrival(s, k).wait_recv()
            c_copy(s, k).start()

    def settle(s):
        for k in range(xs_count):
            c_arrival(s, k).wait_recv()

        def place(at, carry):
            got = gathered[s, at].astype(F32)
            turned = pltpu.roll(got, 64, 3)
            for d in range(xcs):
                by_channel[at, d * cpd : d * cpd + mid, :] = got[d // CORES, d % CORES, 0:mid]
                by_channel[at, d * cpd + mid : (d + 1) * cpd, :] = turned[d // CORES, d % CORES, 0:mid]
            return carry

        lax.fori_loop(0, zs, place, 0)
        span = xcs * cpd
        for ch in range(chunks):
            first, parts = ch * LANES, []
            while first < (ch + 1) * LANES:
                last = min((first // span + 1) * span, (ch + 1) * LANES)
                parts.append(by_channel[first // span, first % span : first % span + last - first, :])
                first = last
            weights[s, ch] = jnp.transpose(jnp.concatenate(parts, axis=0) if len(parts) > 1 else parts[0])[0:64]

    over_z(half)
    lax.fori_loop(0, chunks, clear, 0)
    over_x(half)
    swapped.wait_recv()
    over_z(other)
    own_x.wait()
    widen(half)
    over_core(half)
    over_x(other)
    settle(half)

    def put_halo(pad, halo, s, side, start, first=0, count=chunks):
        def one(ch, carry):
            pad[s, ch, start : start + 3, OFF : OFF + width, :] = halo[s, side, :, :, lanes_of(ch)].astype(F32)
            return carry

        lax.fori_loop(first, first + count, one, 0)

    def par(s, ch, which):
        return weights[s, ch, which : which + 1, :][None]

    inverse_count = 1.0 / channels

    def arrive(s):
        shipped.wait_recv()

        @pl.when(row < rows - 1)
        def _():
            x_down(s).start()

        @pl.when(row > 0)
        def _():
            x_up(s).start()

        widen(s)

    def forward(s):
        @pl.when(row > 0)
        def _():
            x_down(s).wait_recv()
            put_halo(xpad, xhalo, s, 0, 0)

        @pl.when(row < rows - 1)
        def _():
            x_up(s).wait_recv()
            put_halo(xpad, xhalo, s, 1, 3 + height)

        def conv(ch, total):
            acc = jnp.zeros((height, width, LANES), F32) + par(s, ch, BIAS)
            for c in range(7):
                shifted = xpad[s, ch, :, OFF - 3 + c : OFF - 3 + c + width, :]
                for r in range(7):
                    acc = acc + shifted[r : r + height] * par(s, ch, 7 * r + c)
            mixed[s, ch] = acc
            return total + acc

        total = lax.fori_loop(0, chunks, conv, jnp.zeros((height, width, LANES), F32))
        mean = jnp.sum(total, axis=-1, keepdims=True) * inverse_count
        stats[s, 0] = jnp.broadcast_to(mean, (height, width, LANES))
        mean = stats[s, 0]

        def spread(ch, total):
            centred = mixed[s, ch] - mean
            return total + centred * centred

        squares = lax.fori_loop(0, chunks, spread, jnp.zeros((height, width, LANES), F32))
        variance = jnp.sum(squares, axis=-1, keepdims=True) * inverse_count
        inverse = lax.rsqrt(variance + EPSILON)
        stats[s, 1] = jnp.broadcast_to(inverse, (height, width, LANES))

    def folded(value):
        flat_rows = jnp.sum(value, axis=0)
        total = flat_rows[0:8]
        for at in range(8, width, 8):
            total = total + flat_rows[at : at + 8]
        return total

    def norm_back(s):
        @pl.when(s == 1)
        def _():
            own_adj.wait()

        mean = stats[s, 0]
        inverse = stats[s, 1]

        def first(ch, sums):
            normed = (mixed[s, ch] - mean) * inverse
            mixed[s, ch] = normed
            upstream = gbuf[s, :, :, lanes_of(ch)].astype(F32)
            both = upstream * normed
            kacc[ch, SUM_G] = folded(upstream)
            kacc[ch, SUM_GN] = folded(both)
            factor = par(s, ch, SCALE) * par(s, ch, GAIN)
            return sums[0] + upstream * factor, sums[1] + both * factor

        zero = jnp.zeros((height, width, LANES), F32)
        plain, weighted = lax.fori_loop(0, chunks, first, (zero, zero))
        plain = jnp.sum(plain, axis=-1, keepdims=True) * inverse_count
        weighted = jnp.sum(weighted, axis=-1, keepdims=True) * inverse_count

        def second(ch, carry):
            upstream = gbuf[s, :, :, lanes_of(ch)].astype(F32)
            factor = par(s, ch, SCALE) * par(s, ch, GAIN)
            grad = inverse * (upstream * factor - plain - mixed[s, ch] * weighted)
            rounded = grad.astype(BF16)
            gmix[s, :, :, lanes_of(ch)] = rounded
            again = rounded.astype(F32)
            gpad[s, ch, 3 : 3 + height, OFF : OFF + width, :] = again
            kacc[ch, SUM_MIX] = folded(again)
            return carry

        def part(b, carry):
            lax.fori_loop(b * block_chunks, (b + 1) * block_chunks, second, 0)

            @pl.when(row < rows - 1)
            def _():
                g_down(s, b).start()

            @pl.when(row > 0)
            def _():
                g_up(s, b).start()

            return carry

        lax.fori_loop(0, BLOCKS, part, 0)

    def keep_out(s):
        return pltpu.make_async_copy(gbuf.at[1 - s], out_ref.at[half], local_sem.at[2])

    def send_out(s, b):
        return remote(
            gbuf.at[1 - s, :, :, block_of(b)],
            out_ref.at[half, :, :, block_of(b)],
            back_send.at[b],
            back_recv.at[b],
            segment=other,
        )

    def out_arrival(b):
        return remote(
            gbuf.at[0, :, :, block_of(b)],
            out_ref.at[other, :, :, block_of(b)],
            back_send.at[b],
            back_recv.at[b],
            segment=other,
        )

    def adjoint(s):
        def conv(ch, carry):
            acc = gbuf[s, :, :, lanes_of(ch)].astype(F32)
            for c in range(7):
                shifted = gpad[s, ch, :, OFF + 3 - c : OFF + 3 - c + width, :]
                for r in range(7):
                    acc = acc + shifted[6 - r : 6 - r + height] * par(s, ch, 7 * r + c)
            gbuf[1 - s, :, :, lanes_of(ch)] = acc.astype(BF16)
            return carry

        def part(b, carry):
            first = b * block_chunks

            @pl.when(row > 0)
            def _():
                g_down(s, b).wait_recv()
                put_halo(gpad, ghalo, s, 0, 0, first, block_chunks)

            @pl.when(row < rows - 1)
            def _():
                g_up(s, b).wait_recv()
                put_halo(gpad, ghalo, s, 1, 3 + height, first, block_chunks)

            lax.fori_loop(first, first + block_chunks, conv, 0)

            @pl.when(s != half)
            def _():
                send_out(s, b).start()

            return carry

        lax.fori_loop(0, BLOCKS, part, 0)

        @pl.when(s == half)
        def _():
            keep_out(s).start()

    def r1_copy(s, k):
        to = (xc + k) % xcs
        return remote(pieces.at[s, :, to], got1.at[s, xc], r1_send.at[s, k - 1], r1_recv.at[s, xc], dp=dp_of(z, to))

    def r1_arrival(s, k):
        src = (xc + k) % xcs
        return remote(pieces.at[s, :, src], got1.at[s, src], r1_send.at[s, k - 1], r1_recv.at[s, src], dp=dp_of(z, src))

    def taps(s):
        def one(ch, carry):
            grad = gpad[s, ch, 3 : 3 + height, OFF : OFF + width, :]
            for c in range(7):
                shifted = xpad[s, ch, :, OFF - 3 + c : OFF - 3 + c + width, :]
                for r in range(7):
                    kacc[ch, 7 * r + c] = folded(shifted[r : r + height] * grad)
            return carry

        lax.fori_loop(0, chunks, one, 0)

        def total(ch, carry):
            terms[ch] = jnp.zeros((64, LANES), F32)
            for t in range(TAPS + 3):
                terms[ch, t : t + 1, :] = jnp.sum(kacc[ch, t], axis=0, keepdims=True)
            return carry

        lax.fori_loop(0, chunks, total, 0)
        middle = chunks // 2

        for ch in range(middle):
            joined = jnp.concatenate([terms[ch], terms[middle + ch]], axis=0)
            flat[ch * LANES : (ch + 1) * LANES, :] = jnp.transpose(joined)
        for d in range(rows * xcs):
            pieces[s, d // xcs, d % xcs] = flat[d * cpd : (d + 1) * cpd, :]
        for k in range(1, xcs):
            r1_copy(s, k).start()

    ARRIVE, FORWARD, NORM, TAPS_OF, ADJOINT, OVER_CORE, SETTLE = range(7)
    lower = ((ARRIVE, 1), (FORWARD, 0), (OVER_CORE, 1), (SETTLE, 1), (FORWARD, 1), (NORM, 1), (TAPS_OF, 1))
    upper = ((FORWARD, 1), (NORM, 1), (OVER_CORE, 0), (ARRIVE, 0), (TAPS_OF, 1), (SETTLE, 0), (FORWARD, 0))
    common = ((ADJOINT, 1), (NORM, 0), (TAPS_OF, 0), (ADJOINT, 0))
    acts = (arrive, forward, norm_back, taps, adjoint, over_core, settle)

    def digits(order):
        return sum((2 * kind + s) * 16**at for at, (kind, s) in enumerate(order))

    codes = digits(lower) + half * (digits(upper) - digits(lower))

    def step(at, left):
        code = left % 16
        s = code % 2
        for number, act in enumerate(acts):

            @pl.when(code // 2 == number)
            def _():
                act(s)

        return jnp.where(at == len(lower) - 1, digits(common), left // 16)

    lax.fori_loop(0, len(lower) + len(common), step, codes)

    def r2_copy(s, k):
        to = (row + k) % rows
        return remote(
            sum1.at[s, to], got2.at[half, row], r2_send.at[s, k], r2_recv.at[half, row], segment=s, rows=to
        )

    def r2_arrival(k, from_half):
        src = (row + k) % rows
        return remote(
            sum1.at[0, src], got2.at[from_half, src], r2_send.at[0, k], r2_recv.at[from_half, src], segment=other, rows=src
        )

    for s in (1, 0):
        for k in range(1, xcs):
            r1_arrival(s, k).wait_recv()
        got1[s, xc] = pieces[s, :, xc]
        acc = got1[s, 0]
        for k in range(1, xcs):
            acc = acc + got1[s, k]
        sum1[s] = acc

        @pl.when(half == s)
        def _():
            got2[half, row] = sum1[s, row]

        @pl.when(half != s)
        def _():
            r2_copy(s, 0).start()

        for k in range(1, rows):
            r2_copy(s, k).start()

    for k in range(rows):
        if k > 0:
            r2_arrival(k, half).wait_recv()
        r2_arrival(k, other).wait_recv()
    acc = got2[0, 0] + got2[1, 0]
    for k in range(1, rows):
        acc = acc + (got2[0, k] + got2[1, k])
    sum2[...] = acc

    def r3_copy(part, k):
        to_z = part * rows + row
        return remote(sum2, got3.at[z], r3_send.at[part, k], r3_recv.at[z], dp=dp_of(to_z, xc), rows=(row + k) % rows)

    def r3_arrival(k):
        src = (z + k) % zs
        return remote(sum2, got3.at[src], r3_send.at[0, 0], r3_recv.at[src], dp=dp_of(src, xc), rows=zz)

    for part in range(2):
        for k in range(rows):
            if k == 0:

                @pl.when(z != part * rows + row)
                def _():
                    r3_copy(part, 0).start()
            else:
                r3_copy(part, k).start()

    @pl.when(row == zz)
    def _():
        got3[z] = sum2[...]

    @pl.when(row != zz)
    def _():
        r3_arrival(0).wait_recv()

    for k in range(1, zs):
        r3_arrival(k).wait_recv()
    acc = got3[0]
    for k in range(1, zs):
        acc = acc + got3[k]
    scale_by = 1.0 / (2 * zs * xcs)
    sums_ref[...] = jnp.where(z // rows == 1, pltpu.roll(acc, 64, 1), acc) * scale_by

    swap.wait_send()
    ship.wait_send()
    for s in range(2):
        for k in range(1, zs):
            z_copy(s, k).wait_send()
        for k in range(1, xs_count):
            x_copy(s, k).wait_send()
        for k in range(xs_count):
            c_copy(s, k).wait_send()

        @pl.when(row < rows - 1)
        def _():
            x_down(s).wait_send()
            for b in range(BLOCKS):
                g_down(s, b).wait_send()

        @pl.when(row > 0)
        def _():
            x_up(s).wait_send()
            for b in range(BLOCKS):
                g_up(s, b).wait_send()

        for k in range(1, xcs):
            r1_copy(s, k).wait_send()
        for k in range(1, rows):
            r2_copy(s, k).wait_send()

        @pl.when(half != s)
        def _():
            r2_copy(s, 0).wait_send()

    for part in range(2):
        for k in range(rows):
            if k == 0:

                @pl.when(z != part * rows + row)
                def _():
                    r3_copy(part, 0).wait_send()
            else:
                r3_copy(part, k).wait_send()
    keep_out(0).wait()
    for b in range(BLOCKS):
        send_out(0, b).wait_send()
        out_arrival(b).wait_recv()


def finish(whole_ref, sums_ref, gain_ref, shift_ref, scale_ref, out_ref, kgrad_ref, bgrad_ref, ggrad_ref, sgrad_ref, lgrad_ref, held, stage, sem):
    count = held.shape[0]
    fetch = [pltpu.make_async_copy(whole_ref.at[m], held.at[m], sem.at[0, m]) for m in range(count)]
    place = [pltpu.make_async_copy(held.at[m], out_ref.at[m], sem.at[1, m]) for m in range(count)]
    for m in range(count):
        fetch[m].start()
    for m in range(count):
        fetch[m].wait()
        place[m].start()
    cpd = sums_ref.shape[0]
    kgrad_ref[...] = sums_ref[:, 0:TAPS]
    stage[...] = jnp.zeros_like(stage)
    stage[0:cpd, :] = sums_ref[...]
    turned = jnp.transpose(stage[...])
    sum_g = turned[SUM_G : SUM_G + 1, 0:cpd]
    sum_gn = turned[SUM_GN : SUM_GN + 1, 0:cpd]
    bgrad_ref[...] = turned[SUM_MIX : SUM_MIX + 1, 0:cpd]
    own_scale = scale_ref[...].astype(F32)
    ggrad_ref[...] = own_scale * sum_gn
    sgrad_ref[...] = own_scale * sum_g
    lgrad_ref[...] = gain_ref[...].astype(F32) * sum_gn + shift_ref[...].astype(F32) * sum_g
    for m in range(count):
        place[m].wait()


def local(xs_count, section_input, adjoint_in, kernel, conv_bias, ln_gain, ln_shift, layer_scale):
    _, micros, images, height, width, channels = section_input.shape
    cpd = kernel.shape[3]
    rows = lax.axis_size("rows")
    zs = lax.axis_size("dp") // (xs_count * CORES)
    xcs = xs_count * CORES
    chunks = channels // LANES
    vmem = pl.BlockSpec(memory_space=pltpu.VMEM)
    hbm = pl.BlockSpec(memory_space=pltpu.HBM)
    vec = jax.ShapeDtypeStruct((1, cpd), F32)
    dma = pltpu.SemaphoreType.DMA
    scratch = [
        pltpu.VMEM((LANES, LANES), F32),
        pltpu.VMEM((32, LANES), F32),
        pltpu.VMEM((2, zs, xs_count, CORES, 16, LANES), BF16),
        pltpu.VMEM((zs, xcs * cpd, LANES), F32),
        pltpu.VMEM((2, chunks, 64, LANES), F32),
        pltpu.VMEM((2, height, width, channels), BF16),
        pltpu.VMEM((2, 2, 3, width, channels), BF16),
        pltpu.VMEM((2, chunks, height + 6, width + 2 * OFF, LANES), F32),
        pltpu.VMEM((2, chunks, height, width, LANES), F32),
        pltpu.VMEM((2, height, width, channels), BF16),
        pltpu.VMEM((2, height, width, channels), BF16),
        pltpu.VMEM((2, 2, 3, width, channels), BF16),
        pltpu.VMEM((2, chunks, height + 6, width + 2 * OFF, LANES), F32),
        pltpu.VMEM((2, 2, height, width, LANES), F32),
        pltpu.VMEM((chunks, TAPS + 3, 8, LANES), F32),
        pltpu.VMEM((chunks, 64, LANES), F32),
        pltpu.VMEM((channels // 2, LANES), F32),
        pltpu.VMEM((2, rows, xcs, cpd, LANES), F32),
        pltpu.VMEM((2, xcs, rows, cpd, LANES), F32),
        pltpu.VMEM((2, rows, cpd, LANES), F32),
        pltpu.VMEM((2, rows, cpd, LANES), F32),
        pltpu.VMEM((cpd, LANES), F32),
        pltpu.VMEM((zs, cpd, LANES), F32),
        dma((3,)),
        dma((1,)),
        dma((1,)),
        dma((2, zs)),
        dma((2, zs)),
        dma((2, xs_count)),
        dma((2, xs_count)),
        dma((2, xs_count)),
        dma((2, xs_count)),
        dma((1,)),
        dma((1,)),
        dma((2, 2)),
        dma((2, 2)),
        dma((2, 2, BLOCKS)),
        dma((2, 2, BLOCKS)),
        dma((BLOCKS,)),
        dma((BLOCKS,)),
        dma((2, xcs)),
        dma((2, xcs)),
        dma((2, rows)),
        dma((2, rows)),
        dma((2, rows)),
        dma((zs,)),
    ]
    vectors = [vector.reshape(1, cpd) for vector in (conv_bias, ln_gain, ln_shift, layer_scale)]
    whole, sums = pl.pallas_call(
        functools.partial(body, (zs, xs_count, rows, cpd, chunks, height, width)),
        out_shape=(
            jax.ShapeDtypeStruct((micros, height, width, channels), BF16),
            jax.ShapeDtypeStruct((cpd, LANES), F32),
        ),
        in_specs=[hbm, hbm] + [vmem] * 5,
        out_specs=(hbm, vmem),
        scratch_shapes=scratch,
        compiler_params=pltpu.CompilerParams(
            collective_id=0, has_side_effects=True, vmem_limit_bytes=60 * 1024 * 1024
        ),
    )(
        section_input.reshape(micros, height, width, channels),
        adjoint_in.reshape(micros, height, width, channels),
        kernel.reshape(TAPS, cpd).T,
        *vectors,
    )
    adjoint, kgrad, bgrad, ggrad, sgrad, lgrad = pl.pallas_call(
        finish,
        out_shape=(
            jax.ShapeDtypeStruct((micros, height, width, channels), BF16),
            jax.ShapeDtypeStruct((cpd, TAPS), F32),
            vec,
            vec,
            vec,
            vec,
        ),
        in_specs=[hbm] + [vmem] * 4,
        out_specs=(hbm,) + (vmem,) * 5,
        scratch_shapes=[
            pltpu.VMEM((micros, height, width, channels), BF16),
            pltpu.VMEM((LANES, LANES), F32),
            dma((2, micros)),
        ],
        compiler_params=pltpu.CompilerParams(vmem_limit_bytes=60 * 1024 * 1024),
    )(whole, sums, *vectors[1:])
    return (
        adjoint.reshape(section_input.shape),
        kgrad.T.reshape(kernel.shape),
        bgrad.reshape(conv_bias.shape),
        ggrad.reshape(conv_bias.shape),
        sgrad.reshape(conv_bias.shape),
        lgrad.reshape(conv_bias.shape),
    )


def solution(mesh, xs_count=XS):
    placed = (
        P("segment", None, "dp", "rows", None, None),
        P(None, "dp", "rows", None, None),
        P("segment", None, None, "dp"),
        P("segment", None, "dp"),
        P("segment", None, "dp"),
        P("segment", None, "dp"),
        P("segment", None, "dp"),
    )
    return jax.shard_map(
        functools.partial(local, xs_count),
        mesh=mesh,
        in_specs=placed,
        out_specs=(placed[0],) + (placed[2],) + (placed[3],) * 4,
        check_vma=False,
    )
```

```python
import functools

import jax
import jax.numpy as jnp
from jax import lax
from jax.experimental import pallas as pl
from jax.experimental.pallas import tpu as pltpu
from jax.sharding import PartitionSpec as P

MESH = pl.DeviceIdType.MESH
EPSILON = 1e-06
F32 = jnp.float32
BF16 = jnp.bfloat16
LANES = 128
OFF = 8
CORES = 2
XS = 4
TAPS = 49
BIAS, GAIN, SHIFT, SCALE = 49, 50, 51, 52
BLOCKS = 3
SUM_G, SUM_GN, SUM_MIX = 49, 50, 51


def body(
    geometry,
    x_ref,
    adj_ref,
    kern_ref,
    bias_ref,
    gain_ref,
    shift_ref,
    scale_ref,
    out_ref,
    sums_ref,
    stage,
    own,
    gathered,
    by_channel,
    weights,
    xbuf,
    xhalo,
    xpad,
    mixed,
    gbuf,
    gmix,
    ghalo,
    gpad,
    stats,
    kacc,
    terms,
    flat,
    pieces,
    got1,
    sum1,
    got2,
    sum2,
    got3,
    local_sem,
    p_send,
    p_recv,
    z_send,
    z_recv,
    x_send,
    x_recv,
    c_send,
    c_recv,
    ship_send,
    ship_recv,
    xh_send,
    xh_recv,
    gh_send,
    gh_recv,
    back_send,
    back_recv,
    r1_send,
    r1_recv,
    r2_send,
    r2_recv,
    r3_send,
    r3_recv,
):
    zs, xs_count, rows, cpd, chunks, height, width = geometry
    xcs = xs_count * CORES
    channels = chunks * LANES
    half = lax.axis_index("segment")
    other = 1 - half
    dp = lax.axis_index("dp")
    row = lax.axis_index("rows")
    z = dp // xcs
    xc = dp % xcs
    x = xc // CORES
    core = xc % CORES
    zz = z % rows

    def dp_of(z_at, xc_at):
        return z_at * xcs + xc_at

    def remote(src, dst, send, recv, **where):
        return pltpu.make_async_remote_copy(
            src_ref=src, dst_ref=dst, send_sem=send, recv_sem=recv, device_id=where, device_id_type=MESH
        )

    barrier = pltpu.get_barrier_semaphore()

    def greet(**where):
        pl.semaphore_signal(barrier, inc=1, device_id=where, device_id_type=MESH)

    own_x = pltpu.make_async_copy(x_ref.at[half], xbuf.at[half], local_sem.at[0])
    own_adj = pltpu.make_async_copy(adj_ref.at[half], gbuf.at[1], local_sem.at[1])
    own_x.start()
    own_adj.start()

    for k in range(1, zs):
        greet(dp=dp_of((z + k) % zs, xc))
    for k in range(1, xcs):
        greet(dp=dp_of(z, (xc + k) % xcs))
    for k in range(1, rows):
        greet(rows=(row + k) % rows)
    for k in range(rows):
        greet(segment=other, rows=(row + k) % rows)
    for k in range(zs):
        if k == 0:

            @pl.when(row != zz)
            def _():
                greet(rows=zz)
        else:
            greet(dp=dp_of((z + k) % zs, xc), rows=zz)

    stage[...] = jnp.zeros_like(stage)
    stage[BIAS : BIAS + 1, 0:cpd] = bias_ref[...].astype(F32)
    stage[GAIN : GAIN + 1, 0:cpd] = gain_ref[...].astype(F32)
    stage[SHIFT : SHIFT + 1, 0:cpd] = shift_ref[...].astype(F32)
    stage[SCALE : SCALE + 1, 0:cpd] = scale_ref[...].astype(F32)
    vectors = jnp.transpose(stage[...])[0:32]
    own[...] = jnp.zeros_like(own)
    own[0:cpd, 0:TAPS] = kern_ref[...].astype(F32)
    own[...] = own[...] + vectors
    mid = cpd // 2
    gathered[half, z, x, core] = (own[0:16] + pltpu.roll(own[mid : mid + 16], 64, 1)).astype(BF16)

    known = (zs - 1) + (xcs - 1) + (rows - 1) + rows + zs

    @pl.when(row != zz)
    def _():
        pl.semaphore_wait(barrier, known)

    @pl.when(row == zz)
    def _():
        pl.semaphore_wait(barrier, known - 1)

    mine = gathered.at[half, z, x, core]
    swap = remote(mine, mine, p_send.at[0], p_recv.at[0], segment=other)
    swapped = remote(mine, gathered.at[other, z, x, core], p_send.at[0], p_recv.at[0], segment=other)
    swap.start()

    ship = remote(x_ref.at[other], xbuf.at[half], ship_send.at[0], ship_recv.at[0], segment=other)
    shipped = remote(x_ref.at[other], xbuf.at[other], ship_send.at[0], ship_recv.at[0], segment=other)
    ship.start()

    def own_down():
        return remote(x_ref.at[half, height - 3 : height], xhalo.at[half, 0], xh_send.at[half, 0], xh_recv.at[half, 0], rows=(row + 1) % rows)

    def own_up():
        return remote(x_ref.at[half, 0:3], xhalo.at[half, 1], xh_send.at[half, 1], xh_recv.at[half, 1], rows=(row + rows - 1) % rows)

    def x_down(s):
        return remote(xbuf.at[s, height - 3 : height], xhalo.at[s, 0], xh_send.at[s, 0], xh_recv.at[s, 0], rows=(row + 1) % rows)

    def x_up(s):
        return remote(xbuf.at[s, 0:3], xhalo.at[s, 1], xh_send.at[s, 1], xh_recv.at[s, 1], rows=(row + rows - 1) % rows)

    block_chunks = chunks // BLOCKS
    block_lanes = block_chunks * LANES

    def block_of(b):
        return pl.ds(pl.multiple_of(b * block_lanes, LANES), block_lanes)

    def g_down(s, b):
        return remote(
            gmix.at[s, height - 3 : height, :, block_of(b)],
            ghalo.at[s, 0, :, :, block_of(b)],
            gh_send.at[s, 0, b],
            gh_recv.at[s, 0, b],
            rows=(row + 1) % rows,
        )

    def g_up(s, b):
        return remote(
            gmix.at[s, 0:3, :, block_of(b)],
            ghalo.at[s, 1, :, :, block_of(b)],
            gh_send.at[s, 1, b],
            gh_recv.at[s, 1, b],
            rows=(row + rows - 1) % rows,
        )

    @pl.when(row < rows - 1)
    def _():
        own_down().start()

    @pl.when(row > 0)
    def _():
        own_up().start()

    def clear(ch, carry):
        for s in range(2):
            for ref in (xpad, gpad):
                ref[s, ch, :, 0:OFF, :] = jnp.zeros((height + 6, OFF, LANES), F32)
                ref[s, ch, :, OFF + width : 2 * OFF + width, :] = jnp.zeros((height + 6, OFF, LANES), F32)
                ref[s, ch, 0:3, OFF : OFF + width, :] = jnp.zeros((3, width, LANES), F32)
                ref[s, ch, height + 3 : height + 6, OFF : OFF + width, :] = jnp.zeros((3, width, LANES), F32)
        return carry

    def lanes_of(ch):
        return pl.ds(pl.multiple_of(ch * LANES, LANES), LANES)

    def widen(s):
        def one(ch, carry):
            xpad[s, ch, 3 : 3 + height, OFF : OFF + width, :] = xbuf[s, :, :, lanes_of(ch)].astype(F32)
            return carry

        lax.fori_loop(0, chunks, one, 0)

    def z_copy(s, k):
        block = gathered.at[s, z, x, core]
        return remote(block, block, z_send.at[s, k - 1], z_recv.at[s, z], dp=dp_of((z + k) % zs, xc))

    def z_arrival(s, k):
        src = (z + k) % zs
        block = gathered.at[s, src, x, core]
        return remote(block, block, z_send.at[s, k - 1], z_recv.at[s, src], dp=dp_of(src, xc))

    def x_copy(s, k):
        to = (x + k) % xs_count
        block = gathered.at[s, :, x, core]
        return remote(block, block, x_send.at[s, k - 1], x_recv.at[s, x], dp=dp_of(z, to * CORES + core))

    def x_arrival(s, k):
        src = (x + k) % xs_count
        block = gathered.at[s, :, src, core]
        return remote(block, block, x_send.at[s, k - 1], x_recv.at[s, src], dp=dp_of(z, src * CORES + core))

    def c_copy(s, k):
        src = (x + k) % xs_count
        block = gathered.at[s, :, src, core]
        return remote(block, block, c_send.at[s, k], c_recv.at[s, src], dp=dp_of(z, x * CORES + 1 - core))

    def c_arrival(s, k):
        src = (x + k) % xs_count
        block = gathered.at[s, :, src, 1 - core]
        return remote(block, block, c_send.at[s, k], c_recv.at[s, src], dp=dp_of(z, x * CORES + 1 - core))

    def over_z(s):
        for k in range(1, zs):
            z_copy(s, k).start()

    def over_x(s):
        for k in range(1, zs):
            z_arrival(s, k).wait_recv()
        for k in range(1, xs_count):
            x_copy(s, k).start()
        c_copy(s, 0).start()

    def over_core(s):
        for k in range(1, xs_count):
            x_arrival(s, k).wait_recv()
            c_copy(s, k).start()

    def settle(s):
        for k in range(xs_count):
            c_arrival(s, k).wait_recv()

        def place(at, carry):
            got = gathered[s, at].astype(F32)
            turned = pltpu.roll(got, 64, 3)
            for d in range(xcs):
                by_channel[at, d * cpd : d * cpd + mid, :] = got[d // CORES, d % CORES, 0:mid]
                by_channel[at, d * cpd + mid : (d + 1) * cpd, :] = turned[d // CORES, d % CORES, 0:mid]
            return carry

        lax.fori_loop(0, zs, place, 0)
        span = xcs * cpd
        for ch in range(chunks):
            first, parts = ch * LANES, []
            while first < (ch + 1) * LANES:
                last = min((first // span + 1) * span, (ch + 1) * LANES)
                parts.append(by_channel[first // span, first % span : first % span + last - first, :])
                first = last
            weights[s, ch] = jnp.transpose(jnp.concatenate(parts, axis=0) if len(parts) > 1 else parts[0])[0:64]

    over_z(half)
    lax.fori_loop(0, chunks, clear, 0)
    over_x(half)
    swapped.wait_recv()
    over_z(other)
    own_x.wait()
    widen(half)
    over_core(half)
    over_x(other)
    settle(half)

    def put_halo(pad, halo, s, side, start, first=0, count=chunks):
        def one(ch, carry):
            pad[s, ch, start : start + 3, OFF : OFF + width, :] = halo[s, side, :, :, lanes_of(ch)].astype(F32)
            return carry

        lax.fori_loop(first, first + count, one, 0)

    def par(s, ch, which):
        return weights[s, ch, which : which + 1, :][None]

    inverse_count = 1.0 / channels

    def arrive(s):
        shipped.wait_recv()

        @pl.when(row < rows - 1)
        def _():
            x_down(s).start()

        @pl.when(row > 0)
        def _():
            x_up(s).start()

        widen(s)

    def forward(s):
        @pl.when(row > 0)
        def _():
            x_down(s).wait_recv()
            put_halo(xpad, xhalo, s, 0, 0)

        @pl.when(row < rows - 1)
        def _():
            x_up(s).wait_recv()
            put_halo(xpad, xhalo, s, 1, 3 + height)

        def conv(ch, total):
            acc = jnp.zeros((height, width, LANES), F32) + par(s, ch, BIAS)
            for c in range(7):
                shifted = xpad[s, ch, :, OFF - 3 + c : OFF - 3 + c + width, :]
                for r in range(7):
                    acc = acc + shifted[r : r + height] * par(s, ch, 7 * r + c)
            mixed[s, ch] = acc
            return total + acc

        total = lax.fori_loop(0, chunks, conv, jnp.zeros((height, width, LANES), F32))
        mean = jnp.sum(total, axis=-1, keepdims=True) * inverse_count
        stats[s, 0] = jnp.broadcast_to(mean, (height, width, LANES))
        mean = stats[s, 0]

        def spread(ch, total):
            centred = mixed[s, ch] - mean
            return total + centred * centred

        squares = lax.fori_loop(0, chunks, spread, jnp.zeros((height, width, LANES), F32))
        variance = jnp.sum(squares, axis=-1, keepdims=True) * inverse_count
        inverse = lax.rsqrt(variance + EPSILON)
        stats[s, 1] = jnp.broadcast_to(inverse, (height, width, LANES))

    def folded(value):
        flat_rows = jnp.sum(value, axis=0)
        total = flat_rows[0:8]
        for at in range(8, width, 8):
            total = total + flat_rows[at : at + 8]
        return total

    def norm_back(s):
        @pl.when(s == 1)
        def _():
            own_adj.wait()

        mean = stats[s, 0]
        inverse = stats[s, 1]

        def first(ch, sums):
            normed = (mixed[s, ch] - mean) * inverse
            mixed[s, ch] = normed
            upstream = gbuf[s, :, :, lanes_of(ch)].astype(F32)
            both = upstream * normed
            kacc[ch, SUM_G] = folded(upstream)
            kacc[ch, SUM_GN] = folded(both)
            factor = par(s, ch, SCALE) * par(s, ch, GAIN)
            return sums[0] + upstream * factor, sums[1] + both * factor

        zero = jnp.zeros((height, width, LANES), F32)
        plain, weighted = lax.fori_loop(0, chunks, first, (zero, zero))
        plain = jnp.sum(plain, axis=-1, keepdims=True) * inverse_count
        weighted = jnp.sum(weighted, axis=-1, keepdims=True) * inverse_count

        def second(ch, carry):
            upstream = gbuf[s, :, :, lanes_of(ch)].astype(F32)
            factor = par(s, ch, SCALE) * par(s, ch, GAIN)
            grad = inverse * (upstream * factor - plain - mixed[s, ch] * weighted)
            rounded = grad.astype(BF16)
            gmix[s, :, :, lanes_of(ch)] = rounded
            again = rounded.astype(F32)
            gpad[s, ch, 3 : 3 + height, OFF : OFF + width, :] = again
            kacc[ch, SUM_MIX] = folded(again)
            return carry

        def part(b, carry):
            lax.fori_loop(b * block_chunks, (b + 1) * block_chunks, second, 0)

            @pl.when(row < rows - 1)
            def _():
                g_down(s, b).start()

            @pl.when(row > 0)
            def _():
                g_up(s, b).start()

            return carry

        lax.fori_loop(0, BLOCKS, part, 0)

    def keep_out(s):
        return pltpu.make_async_copy(gbuf.at[1 - s], out_ref.at[half], local_sem.at[2])

    def send_out(s, b):
        return remote(
            gbuf.at[1 - s, :, :, block_of(b)],
            out_ref.at[half, :, :, block_of(b)],
            back_send.at[b],
            back_recv.at[b],
            segment=other,
        )

    def out_arrival(b):
        return remote(
            gbuf.at[0, :, :, block_of(b)],
            out_ref.at[other, :, :, block_of(b)],
            back_send.at[b],
            back_recv.at[b],
            segment=other,
        )

    def adjoint(s):
        def conv(ch, carry):
            acc = gbuf[s, :, :, lanes_of(ch)].astype(F32)
            for c in range(7):
                shifted = gpad[s, ch, :, OFF + 3 - c : OFF + 3 - c + width, :]
                for r in range(7):
                    acc = acc + shifted[6 - r : 6 - r + height] * par(s, ch, 7 * r + c)
            gbuf[1 - s, :, :, lanes_of(ch)] = acc.astype(BF16)
            return carry

        def part(b, carry):
            first = b * block_chunks

            @pl.when(row > 0)
            def _():
                g_down(s, b).wait_recv()
                put_halo(gpad, ghalo, s, 0, 0, first, block_chunks)

            @pl.when(row < rows - 1)
            def _():
                g_up(s, b).wait_recv()
                put_halo(gpad, ghalo, s, 1, 3 + height, first, block_chunks)

            lax.fori_loop(first, first + block_chunks, conv, 0)

            @pl.when(s != half)
            def _():
                send_out(s, b).start()

            return carry

        lax.fori_loop(0, BLOCKS, part, 0)

        @pl.when(s == half)
        def _():
            keep_out(s).start()

    def r1_copy(s, k):
        to = (xc + k) % xcs
        return remote(pieces.at[s, :, to], got1.at[s, xc], r1_send.at[s, k - 1], r1_recv.at[s, xc], dp=dp_of(z, to))

    def r1_arrival(s, k):
        src = (xc + k) % xcs
        return remote(pieces.at[s, :, src], got1.at[s, src], r1_send.at[s, k - 1], r1_recv.at[s, src], dp=dp_of(z, src))

    def taps(s):
        def one(ch, carry):
            grad = gpad[s, ch, 3 : 3 + height, OFF : OFF + width, :]
            for c in range(7):
                shifted = xpad[s, ch, :, OFF - 3 + c : OFF - 3 + c + width, :]
                for r in range(7):
                    kacc[ch, 7 * r + c] = folded(shifted[r : r + height] * grad)
            return carry

        lax.fori_loop(0, chunks, one, 0)

        def total(ch, carry):
            terms[ch] = jnp.zeros((64, LANES), F32)
            for t in range(TAPS + 3):
                terms[ch, t : t + 1, :] = jnp.sum(kacc[ch, t], axis=0, keepdims=True)
            return carry

        lax.fori_loop(0, chunks, total, 0)
        middle = chunks // 2

        for ch in range(middle):
            joined = jnp.concatenate([terms[ch], terms[middle + ch]], axis=0)
            flat[ch * LANES : (ch + 1) * LANES, :] = jnp.transpose(joined)
        for pair in range(rows // 2):
            for to in range(xcs):
                owners = [(2 * pair + at) * xcs + to for at in range(2)]
                joined = jnp.concatenate([flat[d * cpd : (d + 1) * cpd, :] for d in owners], axis=0)
                pieces[s, pair, to] = joined.astype(BF16)
        for k in range(1, xcs):
            r1_copy(s, k).start()

    ARRIVE, FORWARD, NORM, TAPS_OF, ADJOINT, OVER_CORE, SETTLE = range(7)
    lower = ((ARRIVE, 1), (FORWARD, 0), (OVER_CORE, 1), (SETTLE, 1), (FORWARD, 1), (NORM, 1), (TAPS_OF, 1))
    upper = ((FORWARD, 1), (NORM, 1), (OVER_CORE, 0), (ARRIVE, 0), (TAPS_OF, 1), (SETTLE, 0), (FORWARD, 0))
    common = ((ADJOINT, 1), (NORM, 0), (TAPS_OF, 0), (ADJOINT, 0))
    acts = (arrive, forward, norm_back, taps, adjoint, over_core, settle)

    def digits(order):
        return sum((2 * kind + s) * 16**at for at, (kind, s) in enumerate(order))

    codes = digits(lower) + half * (digits(upper) - digits(lower))

    def step(at, left):
        code = left % 16
        s = code % 2
        for number, act in enumerate(acts):

            @pl.when(code // 2 == number)
            def _():
                act(s)

        return jnp.where(at == len(lower) - 1, digits(common), left // 16)

    lax.fori_loop(0, len(lower) + len(common), step, codes)

    def r2_copy(s, k):
        to = (row + k) % rows
        return remote(
            sum1.at[s, to], got2.at[half, row], r2_send.at[s, k], r2_recv.at[half, row], segment=s, rows=to
        )

    def r2_arrival(k, from_half):
        src = (row + k) % rows
        return remote(
            sum1.at[0, src], got2.at[from_half, src], r2_send.at[0, k], r2_recv.at[from_half, src], segment=other, rows=src
        )

    for s in (1, 0):
        for k in range(1, xcs):
            r1_arrival(s, k).wait_recv()
        got1[s, xc] = pieces[s, :, xc]
        acc = got1[s, 0].astype(F32)
        for k in range(1, xcs):
            acc = acc + got1[s, k].astype(F32)
        for at in range(rows):
            sum1[s, at] = acc[at // 2, at % 2 * cpd : (at % 2 + 1) * cpd]

        @pl.when(half == s)
        def _():
            got2[half, row] = sum1[s, row]

        @pl.when(half != s)
        def _():
            r2_copy(s, 0).start()

        for k in range(1, rows):
            r2_copy(s, k).start()

    for k in range(rows):
        if k > 0:
            r2_arrival(k, half).wait_recv()
        r2_arrival(k, other).wait_recv()
    acc = got2[0, 0] + got2[1, 0]
    for k in range(1, rows):
        acc = acc + (got2[0, k] + got2[1, k])
    sum2[...] = acc

    def r3_copy(part, k):
        to_z = part * rows + row
        return remote(sum2, got3.at[z], r3_send.at[part, k], r3_recv.at[z], dp=dp_of(to_z, xc), rows=(row + k) % rows)

    def r3_arrival(k):
        src = (z + k) % zs
        return remote(sum2, got3.at[src], r3_send.at[0, 0], r3_recv.at[src], dp=dp_of(src, xc), rows=zz)

    for part in range(2):
        for k in range(rows):
            if k == 0:

                @pl.when(z != part * rows + row)
                def _():
                    r3_copy(part, 0).start()
            else:
                r3_copy(part, k).start()

    @pl.when(row == zz)
    def _():
        got3[z] = sum2[...]

    @pl.when(row != zz)
    def _():
        r3_arrival(0).wait_recv()

    for k in range(1, zs):
        r3_arrival(k).wait_recv()
    acc = got3[0]
    for k in range(1, zs):
        acc = acc + got3[k]
    scale_by = 1.0 / (2 * zs * xcs)
    sums_ref[...] = jnp.where(z // rows == 1, pltpu.roll(acc, 64, 1), acc) * scale_by

    swap.wait_send()
    ship.wait_send()
    for s in range(2):
        for k in range(1, zs):
            z_copy(s, k).wait_send()
        for k in range(1, xs_count):
            x_copy(s, k).wait_send()
        for k in range(xs_count):
            c_copy(s, k).wait_send()

        @pl.when(row < rows - 1)
        def _():
            x_down(s).wait_send()
            for b in range(BLOCKS):
                g_down(s, b).wait_send()

        @pl.when(row > 0)
        def _():
            x_up(s).wait_send()
            for b in range(BLOCKS):
                g_up(s, b).wait_send()

        for k in range(1, xcs):
            r1_copy(s, k).wait_send()
        for k in range(1, rows):
            r2_copy(s, k).wait_send()

        @pl.when(half != s)
        def _():
            r2_copy(s, 0).wait_send()

    for part in range(2):
        for k in range(rows):
            if k == 0:

                @pl.when(z != part * rows + row)
                def _():
                    r3_copy(part, 0).wait_send()
            else:
                r3_copy(part, k).wait_send()
    keep_out(0).wait()
    for b in range(BLOCKS):
        send_out(0, b).wait_send()
        out_arrival(b).wait_recv()


def finish(whole_ref, sums_ref, gain_ref, shift_ref, scale_ref, out_ref, kgrad_ref, bgrad_ref, ggrad_ref, sgrad_ref, lgrad_ref, held, stage, sem):
    count = held.shape[0]
    fetch = [pltpu.make_async_copy(whole_ref.at[m], held.at[m], sem.at[0, m]) for m in range(count)]
    place = [pltpu.make_async_copy(held.at[m], out_ref.at[m], sem.at[1, m]) for m in range(count)]
    for m in range(count):
        fetch[m].start()
    for m in range(count):
        fetch[m].wait()
        place[m].start()
    cpd = sums_ref.shape[0]
    kgrad_ref[...] = sums_ref[:, 0:TAPS]
    stage[...] = jnp.zeros_like(stage)
    stage[0:cpd, :] = sums_ref[...]
    turned = jnp.transpose(stage[...])
    sum_g = turned[SUM_G : SUM_G + 1, 0:cpd]
    sum_gn = turned[SUM_GN : SUM_GN + 1, 0:cpd]
    bgrad_ref[...] = turned[SUM_MIX : SUM_MIX + 1, 0:cpd]
    own_scale = scale_ref[...].astype(F32)
    ggrad_ref[...] = own_scale * sum_gn
    sgrad_ref[...] = own_scale * sum_g
    lgrad_ref[...] = gain_ref[...].astype(F32) * sum_gn + shift_ref[...].astype(F32) * sum_g
    for m in range(count):
        place[m].wait()


def local(xs_count, section_input, adjoint_in, kernel, conv_bias, ln_gain, ln_shift, layer_scale):
    _, micros, images, height, width, channels = section_input.shape
    cpd = kernel.shape[3]
    rows = lax.axis_size("rows")
    zs = lax.axis_size("dp") // (xs_count * CORES)
    xcs = xs_count * CORES
    chunks = channels // LANES
    vmem = pl.BlockSpec(memory_space=pltpu.VMEM)
    hbm = pl.BlockSpec(memory_space=pltpu.HBM)
    vec = jax.ShapeDtypeStruct((1, cpd), F32)
    dma = pltpu.SemaphoreType.DMA
    scratch = [
        pltpu.VMEM((LANES, LANES), F32),
        pltpu.VMEM((32, LANES), F32),
        pltpu.VMEM((2, zs, xs_count, CORES, 16, LANES), BF16),
        pltpu.VMEM((zs, xcs * cpd, LANES), F32),
        pltpu.VMEM((2, chunks, 64, LANES), F32),
        pltpu.VMEM((2, height, width, channels), BF16),
        pltpu.VMEM((2, 2, 3, width, channels), BF16),
        pltpu.VMEM((2, chunks, height + 6, width + 2 * OFF, LANES), F32),
        pltpu.VMEM((2, chunks, height, width, LANES), F32),
        pltpu.VMEM((2, height, width, channels), BF16),
        pltpu.VMEM((2, height, width, channels), BF16),
        pltpu.VMEM((2, 2, 3, width, channels), BF16),
        pltpu.VMEM((2, chunks, height + 6, width + 2 * OFF, LANES), F32),
        pltpu.VMEM((2, 2, height, width, LANES), F32),
        pltpu.VMEM((chunks, TAPS + 3, 8, LANES), F32),
        pltpu.VMEM((chunks, 64, LANES), F32),
        pltpu.VMEM((channels // 2, LANES), F32),
        pltpu.VMEM((2, rows // 2, xcs, 2 * cpd, LANES), BF16),
        pltpu.VMEM((2, xcs, rows // 2, 2 * cpd, LANES), BF16),
        pltpu.VMEM((2, rows, cpd, LANES), F32),
        pltpu.VMEM((2, rows, cpd, LANES), F32),
        pltpu.VMEM((cpd, LANES), F32),
        pltpu.VMEM((zs, cpd, LANES), F32),
        dma((3,)),
        dma((1,)),
        dma((1,)),
        dma((2, zs)),
        dma((2, zs)),
        dma((2, xs_count)),
        dma((2, xs_count)),
        dma((2, xs_count)),
        dma((2, xs_count)),
        dma((1,)),
        dma((1,)),
        dma((2, 2)),
        dma((2, 2)),
        dma((2, 2, BLOCKS)),
        dma((2, 2, BLOCKS)),
        dma((BLOCKS,)),
        dma((BLOCKS,)),
        dma((2, xcs)),
        dma((2, xcs)),
        dma((2, rows)),
        dma((2, rows)),
        dma((2, rows)),
        dma((zs,)),
    ]
    vectors = [vector.reshape(1, cpd) for vector in (conv_bias, ln_gain, ln_shift, layer_scale)]
    whole, sums = pl.pallas_call(
        functools.partial(body, (zs, xs_count, rows, cpd, chunks, height, width)),
        out_shape=(
            jax.ShapeDtypeStruct((micros, height, width, channels), BF16),
            jax.ShapeDtypeStruct((cpd, LANES), F32),
        ),
        in_specs=[hbm, hbm] + [vmem] * 5,
        out_specs=(hbm, vmem),
        scratch_shapes=scratch,
        compiler_params=pltpu.CompilerParams(
            collective_id=0, has_side_effects=True, vmem_limit_bytes=60 * 1024 * 1024
        ),
    )(
        section_input.reshape(micros, height, width, channels),
        adjoint_in.reshape(micros, height, width, channels),
        kernel.reshape(TAPS, cpd).T,
        *vectors,
    )
    adjoint, kgrad, bgrad, ggrad, sgrad, lgrad = pl.pallas_call(
        finish,
        out_shape=(
            jax.ShapeDtypeStruct((micros, height, width, channels), BF16),
            jax.ShapeDtypeStruct((cpd, TAPS), F32),
            vec,
            vec,
            vec,
            vec,
        ),
        in_specs=[hbm] + [vmem] * 4,
        out_specs=(hbm,) + (vmem,) * 5,
        scratch_shapes=[
            pltpu.VMEM((micros, height, width, channels), BF16),
            pltpu.VMEM((LANES, LANES), F32),
            dma((2, micros)),
        ],
        compiler_params=pltpu.CompilerParams(vmem_limit_bytes=60 * 1024 * 1024),
    )(whole, sums, *vectors[1:])
    return (
        adjoint.reshape(section_input.shape),
        kgrad.T.reshape(kernel.shape),
        bgrad.reshape(conv_bias.shape),
        ggrad.reshape(conv_bias.shape),
        sgrad.reshape(conv_bias.shape),
        lgrad.reshape(conv_bias.shape),
    )


def solution(mesh, xs_count=XS):
    placed = (
        P("segment", None, "dp", "rows", None, None),
        P(None, "dp", "rows", None, None),
        P("segment", None, None, "dp"),
        P("segment", None, "dp"),
        P("segment", None, "dp"),
        P("segment", None, "dp"),
        P("segment", None, "dp"),
    )
    return jax.shard_map(
        functools.partial(local, xs_count),
        mesh=mesh,
        in_specs=placed,
        out_specs=(placed[0],) + (placed[2],) + (placed[3],) * 4,
        check_vma=False,
    )
```
